32 devices in a mesh: groups: 2 (over y), fsdp: 4 (over z), tp: 2 (over x), dp: 2 (over core).
Axes of the slice: x: 2, y: 2, z: 4, core: 2. Of those that a mesh axis runs over, the one named last changes fastest.
Arguments:
- activations: bfloat16 [5120, 8192], P(('groups', 'fsdp'), ('tp', 'dp')), parts along dimension 0, may hold values from -6 to 6
- grad_out: bfloat16 [5120, 2048], P(('groups', 'fsdp')), parts along dimension 0, may hold values from -6 to 6
- codes: bfloat16 [8192, 2048], P(('tp', 'dp'), 'fsdp'), may hold values from -0.125 to 0.125
- scales: float32 [64, 16], P(('tp', 'dp')), may hold values from 0.5 to 2
- adapter_a: bfloat16 [4, 8192, 128], P('fsdp', ('tp', 'dp')), may hold values from -0.0625 to 0.0625
- adapter_b: bfloat16 [4, 2048, 64], P('fsdp', ('tp', 'dp')), may hold values from -0.1875 to 0.1875
- lengths: int32 [8], P('groups'), parts along dimension 0, may hold values from 160 to 1920, as said below
- slot_job: int32 [4], replicated, may hold values from 0 to 3, each once
Outputs:
- input_gradient: bfloat16 [5120, 8192], P(('groups', 'fsdp'), ('tp', 'dp')), parts along dimension 0
- grad_a: float32 [8, 8192, 128], P(('groups', 'fsdp'), ('tp', 'dp')), parts along dimension 0
- grad_b: float32 [8, 2048, 64], P(('groups', 'fsdp'), ('tp', 'dp')), parts along dimension 0
The draws below stay inside these ranges and needn't reach their ends.
There are 2 independent parts, one for each index of `groups`. The reference program is written for one: setup_inputs(seed, part) draws one part's arguments, and reference() takes and returns one part's arrays. A program takes and returns all parts, laid end to end along the dimension named above; an argument that names none is the same for every part. Nothing has to cross between parts.
Inputs may be any that keep to these rules, and one draw needn't show every extreme that they name: The longest job has exactly 1920 rows and the shortest exactly 160; the lengths sum to 2560. `slot_job`: each job appears in exactly one slot.
All inputs are finite; a program needn't handle non-finite values.
Results may differ from the reference program's by a relative error of at most 0.015.
Values may be sent and summed in bfloat16 or wider, within the bound.
No kernel may reach another device: no remote copies, remote signals or barrier semaphores. Data moves between devices by JAX's collectives and lax.ppermute only.
A program may use at most 128 MiB of HBM per device.

```python
import math
import jax
import jax.numpy as jnp
from jax import lax

D = 8192
HV = 1024
RANK = 64
BLOCK = 128
TOK_DEV = 640
JOBS = 4
TOKENS = 2560
N_FSDP = 4


def draw_lengths(key, part):
    key = jax.random.fold_in(key, 7)
    shortest = TOK_DEV // 4
    longest = 3 * TOK_DEV
    rest = JOBS - 2
    spare = TOKENS - longest - (JOBS - 1) * shortest
    key_weight, key_order = jax.random.split(key)
    weights = jax.random.randint(key_weight, (rest,), 2, 6, dtype=jnp.int32)
    running = jnp.cumsum(weights)
    total = running[rest - 1]
    marks = spare * running // total
    extra = marks - jnp.concatenate([jnp.zeros((1,), jnp.int32), marks[:rest - 1]])
    values = jnp.concatenate([jnp.array([longest, shortest], jnp.int32), extra + shortest])
    return jax.random.permutation(key_order, values).astype(jnp.int32)


def block_scale(rng, extent, cuts, smallest, largest):
    level, own = 1.0, jax.random.fold_in(rng, 6)
    for position, parts in cuts:
        steps = jnp.exp(jax.random.uniform(jax.random.fold_in(own, position), (parts,), jnp.float32, smallest / len(cuts), largest / len(cuts)))
        level = level * jnp.repeat(steps, extent[position] // parts).reshape([-1 if axis == position else 1 for axis in range(len(extent))])
    return level


def centred(stream_key, dims, scale, reach, pieces=(), held_as=jnp.bfloat16):
    values = jax.random.normal(stream_key, dims, jnp.float32) * scale
    if len(pieces) > 0:
        values = block_scale(stream_key, dims, pieces, -0.22, 0.18) * values
    return jnp.clip(values, min=-reach, max=reach).astype(held_as)


def setup_inputs(seed: int = 0, part: int = 0) -> dict:
    splits = jax.random.split(jax.random.key(seed), 9)
    own_keys = jax.random.split(jax.random.fold_in(splits[8], part), 9)
    return {
        "activations": centred(own_keys[0], (TOKENS, D), 1.0, 6.0, ((0, 4), (1, 4))),
        "grad_out": centred(own_keys[1], (TOKENS, 2 * HV), 1.0, 6.0, ((0, 4),)),
        "codes": centred(splits[2], (D, 2 * HV), (2 * HV) ** -0.5, 0.125, ((0, 4), (1, 4))),
        "scales": jnp.clip(jnp.exp(math.log(2.0) - 1.3862944 * jax.random.uniform(splits[3], (D // BLOCK, 2 * HV // BLOCK), jnp.float32) ** block_scale(splits[3], (D // BLOCK, 2 * HV // BLOCK), ((0, 4),), -0.2, 0.2)), 0.5, 2.0),
        "adapter_a": centred(splits[4], (JOBS, D, 2 * RANK), D ** -0.5, 0.0625, ((0, 4), (1, 4))),
        "adapter_b": centred(splits[5], (JOBS, 2 * HV, RANK), HV ** -0.5, 0.1875, ((0, 4), (1, 4))),
        "lengths": draw_lengths(jax.random.fold_in(jax.random.fold_in(splits[8], part), 71), part),
        "slot_job": jax.random.permutation(splits[7], JOBS).astype(jnp.int32),
    }


adapter_scale = 2.0


def row_jobs(lengths, total):
    starts = jnp.cumsum(lengths) - lengths
    positions = jnp.arange(total, dtype=jnp.int32)
    return jnp.sum((positions[:, None] >= starts[None, :]).astype(jnp.int32), axis=1) - 1


def reference(activations, grad_out, codes, scales, adapter_a, adapter_b, lengths, slot_job):
    inverse = jnp.argsort(slot_job)
    a_job = adapter_a[inverse]
    b_job = adapter_b[inverse]
    scale_full = jnp.repeat(jnp.repeat(scales, BLOCK, axis=0), BLOCK, axis=1)
    weight = (codes.astype(jnp.float32) * scale_full).astype(jnp.bfloat16)
    frozen_term = lax.dot_general(grad_out, weight, (((1,), (1,)), ((), ())), preferred_element_type=jnp.float32)
    sizes_job = lengths.astype(jnp.int32)
    low_h = lax.ragged_dot(activations, a_job, sizes_job, preferred_element_type=jnp.float32).astype(jnp.bfloat16)
    u_key = lax.ragged_dot(grad_out[:, :HV], b_job[:, :HV, :], sizes_job, preferred_element_type=jnp.float32)
    u_val = lax.ragged_dot(grad_out[:, HV:], b_job[:, HV:, :], sizes_job, preferred_element_type=jnp.float32)
    low_u = jnp.concatenate([u_key, u_val], axis=1).astype(jnp.bfloat16)
    adapter_branch = lax.ragged_dot(low_u, jnp.swapaxes(a_job, 1, 2), sizes_job, preferred_element_type=jnp.float32)
    input_gradient = (frozen_term + adapter_scale * adapter_branch).astype(jnp.bfloat16)

    jobs = row_jobs(lengths, TOKENS)
    onehot = (jobs[:, None] == slot_job[None, :]).astype(jnp.bfloat16)

    def block_terms(carry, index):
        total_a, total_b = carry
        first = (index * TOK_DEV).astype(jnp.int32)
        input_rows = lax.dynamic_slice_in_dim(activations, first, TOK_DEV, 0)
        g_rows = lax.dynamic_slice_in_dim(grad_out, first, TOK_DEV, 0)
        m_rows = lax.dynamic_slice_in_dim(onehot, first, TOK_DEV, 0)
        u_rows = lax.dynamic_slice_in_dim(low_u, first, TOK_DEV, 0)
        h_rows = lax.dynamic_slice_in_dim(low_h, first, TOK_DEV, 0)
        masked_update = (m_rows[:, :, None] * u_rows[:, None, :]).reshape(TOK_DEV, JOBS * 2 * RANK)
        down_portion = lax.dot_general(input_rows, masked_update, (((0,), (0,)), ((), ())), preferred_element_type=jnp.float32) * adapter_scale
        masked_key = (m_rows[:, :, None] * h_rows[:, None, :RANK]).reshape(TOK_DEV, JOBS * RANK)
        masked_val = (m_rows[:, :, None] * h_rows[:, None, RANK:]).reshape(TOK_DEV, JOBS * RANK)
        key_portion = lax.dot_general(g_rows[:, :HV], masked_key, (((0,), (0,)), ((), ())), preferred_element_type=jnp.float32)
        value_portion = lax.dot_general(g_rows[:, HV:], masked_val, (((0,), (0,)), ((), ())), preferred_element_type=jnp.float32)
        up_portion = jnp.concatenate([key_portion, value_portion], axis=0) * adapter_scale
        down_portion = lax.optimization_barrier(down_portion.astype(jnp.bfloat16)).astype(jnp.float32)
        up_portion = lax.optimization_barrier(up_portion.astype(jnp.bfloat16)).astype(jnp.float32)
        return (total_a + down_portion, total_b + up_portion), None

    start_a = jnp.zeros((D, JOBS * 2 * RANK), jnp.float32)
    start_b = jnp.zeros((2 * HV, JOBS * RANK), jnp.float32)
    (total_a, total_b), _ = lax.scan(block_terms, (start_a, start_b), jnp.arange(N_FSDP, dtype=jnp.int32))
    grad_a = jnp.transpose(total_a.reshape(D, JOBS, 2 * RANK), (1, 0, 2))
    grad_b = jnp.transpose(total_b.reshape(2 * HV, JOBS, RANK), (1, 0, 2))
    return input_gradient, grad_a, grad_b
```

```python
import functools
import jax
import jax.numpy as jnp
from jax import lax
from jax.experimental import pallas as pl
from jax.experimental.pallas import tpu as pltpu
from jax.sharding import PartitionSpec as P

BLOCK = 128
CHUNKS = 2

adapter_scale = 2.0

ANY = pl.BlockSpec(memory_space=pl.ANY)
SMEM = pl.BlockSpec(memory_space=pltpu.SMEM)
VMEM = pl.BlockSpec(memory_space=pltpu.VMEM)
VMEM_LIMIT = 48 * 1024 * 1024


def swap_pairs(size):
    return [(k, (k + 1) % size) for k in range(size)]


def spread(x, n):
    from_left = lax.ppermute(x, "fsdp", [(k, k + 1) for k in range(n - 1)])
    from_right = lax.ppermute(x, "fsdp", [(k + 1, k) for k in range(n - 1)])
    across = lax.ppermute(x, "fsdp", [(k, (k + 2) % n) for k in range(n)])
    ends = lax.ppermute(across, "fsdp", [(1, 0), (n - 2, n - 1)])
    return from_left, from_right, across, ends


def swap_groups(blocks, n):
    holders = (range(1, n), range(0, n - 1), range(n), (0, n - 1))
    return tuple(
        lax.ppermute(block, ("groups", "fsdp"), [(g * n + k, (1 - g) * n + k) for g in range(2) for k in held])
        for block, held in zip(blocks, holders)
    )


def chain_scatter(terms, f, n):
    total = lax.dynamic_index_in_dim(terms, f, 0, keepdims=False).astype(jnp.float32)
    leftward = rightward = None
    for t in range(1, n):
        x = lax.dynamic_index_in_dim(terms, jnp.clip(f - n + t, 0, n - 1), 0, keepdims=False)
        x = x if leftward is None else x + leftward
        leftward = lax.ppermute(x, "fsdp", [(k, k - 1) for k in range(n - t, n)])
        y = lax.dynamic_index_in_dim(terms, jnp.clip(f + n - t, 0, n - 1), 0, keepdims=False)
        y = y if rightward is None else y + rightward
        rightward = lax.ppermute(y, "fsdp", [(k, k + 1) for k in range(t)])
    return total + leftward.astype(jnp.float32) + rightward.astype(jnp.float32)


def pick(slot, f, n, own, blocks, act):
    from_left, from_right, across, ends = blocks
    pl.when(f == slot)(lambda: act(own))
    pl.when(lax.rem(f + 2, n) == slot)(lambda: act(across))
    if slot == n - 1:
        pl.when(f == 0)(lambda: act(ends))
    if slot == 0:
        pl.when(f == n - 1)(lambda: act(ends))
    if slot < n - 1:
        pl.when(f == slot + 1)(lambda: act(from_left))
    if slot > 0:
        pl.when(f == slot - 1)(lambda: act(from_right))


def slot_bounds(slot, lengths, slot_job, first):
    job = slot_job[slot]
    start = jnp.int32(0)
    for j in range(lengths.shape[0]):
        start = start + jnp.where(j < job, lengths[j], 0)
    return start - first, start - first + lengths[job]


def row_mask(slot, lengths, slot_job, first, shape):
    low, high = slot_bounds(slot, lengths, slot_job, first)
    row = lax.broadcasted_iota(jnp.int32, shape, 0)
    return (row >= low) & (row < high)


NT = (((1,), (1,)), ((), ()))
TN = (((0,), (0,)), ((), ()))


def u_kernel(n, ids, lengths, slot_job, grad, own, *refs):
    blocks, (out, g_all, b_all, sems) = refs[:4], refs[4:]
    f, column = ids[0], ids[2]
    rows, cols = g_all.shape
    rank = out.shape[1]
    grab = pltpu.make_async_copy(grad.at[:, pl.ds(pl.multiple_of(column * cols, cols), cols)], g_all, sems.at[n])
    grab.start()
    for s in range(n):
        pick(s, f, n, own, blocks, lambda ref, s=s: pltpu.make_async_copy(ref, b_all.at[pl.ds(s * rank, rank)], sems.at[s]).start())
    for s in range(n):
        pltpu.make_async_copy(own, b_all.at[pl.ds(s * rank, rank)], sems.at[s]).wait()
    grab.wait()
    total = jnp.zeros(out.shape, jnp.float32)
    for s in range(n):
        part = lax.dot_general(g_all[...], b_all[s * rank:(s + 1) * rank, :], NT, preferred_element_type=jnp.float32)
        total = jnp.where(row_mask(s, lengths, slot_job, f * rows, out.shape), part, total)
    out[...] = total


def h_kernel(n, ids, lengths, slot_job, acts, own, *refs):
    blocks, swapped, (out, a_out, a_all, sems, out_sem) = refs[:4], refs[4:8], refs[8:]
    f, g = ids[0], ids[1]
    rows = acts.shape[0]
    half = blocks[0].shape[0]
    both = out.shape[1]
    for s in range(n):
        for side, held in enumerate((blocks, swapped)):
            first = pl.multiple_of(jnp.where(side == 0, g, 1 - g) * half, half)
            dst = a_all.at[pl.ds(first, half), pl.ds(s * both, both)]
            pick(s, f, n, own.at[pl.ds(first, half)], held, lambda ref, dst=dst, s=s, side=side: pltpu.make_async_copy(ref, dst, sems.at[s, side]).start())
    for s in range(n):
        for side in range(2):
            dst = a_all.at[pl.ds(0, half), pl.ds(s * both, both)]
            pltpu.make_async_copy(blocks[0], dst, sems.at[s, side]).wait()
    keep = pltpu.make_async_copy(a_all, a_out, out_sem)
    keep.start()
    product = jnp.dot(acts[...], a_all[...], preferred_element_type=jnp.float32)
    total = jnp.zeros(out.shape, jnp.float32)
    for s in range(n):
        total = jnp.where(row_mask(s, lengths, slot_job, f * rows, out.shape), product[:, s * both:(s + 1) * both], total)
    out[...] = total
    keep.wait()


def terms_a_kernel(n, ids, lengths, slot_job, acts, low_u, out, masked):
    f = ids[0]
    rows, both = low_u.shape
    doubled = low_u[...].astype(jnp.float32) * adapter_scale
    for s in range(n):
        part = jnp.where(row_mask(s, lengths, slot_job, f * rows, low_u.shape), doubled, 0.0).astype(jnp.bfloat16)
        masked[:, s * both:(s + 1) * both] = part
        out[s] = lax.dot_general(acts[...], part, TN, preferred_element_type=jnp.float32).astype(jnp.bfloat16)


def terms_b_kernel(n, ids, lengths, slot_job, grad, h_side, out, g_all, sem):
    f, column = ids[0], ids[2]
    rows, cols = g_all.shape
    grab = pltpu.make_async_copy(grad.at[:, pl.ds(pl.multiple_of(column * cols, cols), cols)], g_all, sem)
    grab.start()
    doubled = h_side[...].astype(jnp.float32) * adapter_scale
    grab.wait()
    for s in range(n):
        part = jnp.where(row_mask(s, lengths, slot_job, f * rows, h_side.shape), doubled, 0.0).astype(jnp.bfloat16)
        out[s] = lax.dot_general(part, g_all[...], TN, preferred_element_type=jnp.float32).astype(jnp.bfloat16)


def base_kernel(n, chunk, ids, grad, masked, scale_rows, a_all, own, *refs):
    blocks, swapped = refs[:4], refs[4:8]
    out, codes, factors, result, sems, a_sems, out_sems = refs[-7:]
    f, g = ids[0], ids[1]
    size, cols = blocks[0].shape
    half = own.shape[0] // 2
    firsts = []
    for side, held in enumerate((blocks, swapped)):
        first = pl.multiple_of(jnp.where(side == 0, g, 1 - g) * half + chunk * size, size)
        firsts.append(first)
        for s in range(n):
            dst = codes.at[side, :, pl.ds(s * cols, cols)]
            pick(s, f, n, own.at[pl.ds(first, size)], held, lambda ref, dst=dst, s=s, side=side: pltpu.make_async_copy(ref, dst, sems.at[side, s]).start())
        pltpu.make_async_copy(a_all.at[pl.ds(first, size)], factors.at[side], a_sems.at[side]).start()
    for side in range(2):
        first = firsts[side]
        for s in range(n):
            pltpu.make_async_copy(blocks[0], codes.at[side, :, pl.ds(s * cols, cols)], sems.at[side, s]).wait()
        pltpu.make_async_copy(a_all.at[pl.ds(first, size)], factors.at[side], a_sems.at[side]).wait()
        weight = []
        for b in range(size // BLOCK):
            scale = scale_rows[pl.ds(first // BLOCK + b, 1), :]
            weight.append((codes[side, b * BLOCK:(b + 1) * BLOCK, :].astype(jnp.float32) * scale).astype(jnp.bfloat16))
        weight = jnp.concatenate(weight, axis=0)
        total = lax.dot_general(grad[...], weight, NT, preferred_element_type=jnp.float32)
        total += lax.dot_general(masked[...], factors[side], NT, preferred_element_type=jnp.float32)
        result[side] = total.astype(jnp.bfloat16)
        pltpu.make_async_copy(result.at[side], out.at[:, pl.ds(first, size)], out_sems.at[side]).start()
    for side in range(2):
        pltpu.make_async_copy(result.at[side], out.at[:, pl.ds(firsts[side], size)], out_sems.at[side]).wait()


def params():
    return pltpu.CompilerParams(vmem_limit_bytes=VMEM_LIMIT)


def cost(flops, moved):
    return pl.CostEstimate(flops=int(flops), bytes_accessed=int(moved), transcendentals=0)


def local_chain(activations, grad_out, codes, scales, adapter_a, adapter_b, lengths, slot_job):
    n = 4
    rows, width = activations.shape
    wide = grad_out.shape[1]
    both = adapter_a.shape[2]
    rank = both // 2
    cols = codes.shape[1]
    block_cols = adapter_b.shape[1]
    half = width // 2
    f, g = lax.axis_index("fsdp"), lax.axis_index("groups")
    tp, dp = lax.axis_index("tp"), lax.axis_index("dp")
    ids = jnp.stack([f, g, tp * 2 + dp]).astype(jnp.int32)
    a_own = adapter_a[0]
    b_own = adapter_b[0].T

    b_blocks = spread(b_own, n)
    a_half = lax.dynamic_slice_in_dim(a_own, g * half, half, 0)
    a_blocks = spread(a_half, n)
    a_swapped = swap_groups(a_blocks, n)
    size = half // CHUNKS
    code_blocks, code_swapped = [], []
    for c in range(CHUNKS):
        piece = lax.dynamic_slice_in_dim(codes, g * half + c * size, size, 0)
        got = spread(piece, n)
        code_blocks.append(got)
        code_swapped.append(swap_groups(got, n))

    u_part = pl.pallas_call(
        functools.partial(u_kernel, n),
        out_shape=jax.ShapeDtypeStruct((rows, rank), jnp.float32),
        in_specs=[SMEM] * 3 + [ANY] * 6,
        out_specs=VMEM,
        scratch_shapes=[
            pltpu.VMEM((rows, block_cols), jnp.bfloat16),
            pltpu.VMEM((n * rank, block_cols), jnp.bfloat16),
            pltpu.SemaphoreType.DMA((n + 1,)),
        ],
        compiler_params=params(),
        cost_estimate=cost(2 * rows * block_cols * n * rank, rows * block_cols * 2),
        name="low_u",
    )(ids, lengths, slot_job, grad_out, b_own, *b_blocks)
    u_own = (u_part + lax.ppermute(u_part, "dp", swap_pairs(2))).astype(jnp.bfloat16)
    u_far = lax.ppermute(u_own, "tp", swap_pairs(2))
    low_u = jnp.where(tp == 0, jnp.concatenate([u_own, u_far], axis=1), jnp.concatenate([u_far, u_own], axis=1))

    terms_a, masked_u = pl.pallas_call(
        functools.partial(terms_a_kernel, n),
        out_shape=(
            jax.ShapeDtypeStruct((n, width, both), jnp.bfloat16),
            jax.ShapeDtypeStruct((rows, n * both), jnp.bfloat16),
        ),
        in_specs=[SMEM] * 3 + [VMEM] * 2,
        out_specs=(VMEM, VMEM),
        compiler_params=params(),
        cost_estimate=cost(2 * rows * width * n * both, rows * width * 2 + n * width * both * 2),
        name="terms_a",
    )(ids, lengths, slot_job, activations, low_u)
    grad_a = chain_scatter(terms_a, f, n)

    h_part, a_all = pl.pallas_call(
        functools.partial(h_kernel, n),
        out_shape=(
            jax.ShapeDtypeStruct((rows, both), jnp.float32),
            jax.ShapeDtypeStruct((width, n * both), jnp.bfloat16),
        ),
        in_specs=[SMEM] * 3 + [VMEM] + [ANY] * 9,
        out_specs=(VMEM, ANY),
        scratch_shapes=[
            pltpu.VMEM((width, n * both), jnp.bfloat16),
            pltpu.SemaphoreType.DMA((n, 2)),
            pltpu.SemaphoreType.DMA,
        ],
        compiler_params=params(),
        cost_estimate=cost(2 * rows * width * n * both, rows * width * 2 + n * width * both * 4),
        name="low_h",
    )(ids, lengths, slot_job, activations, a_own, *a_blocks, *a_swapped)
    h_core = (h_part + lax.ppermute(h_part, "dp", swap_pairs(2))).astype(jnp.bfloat16)
    low_h = h_core + lax.ppermute(h_core, "tp", swap_pairs(2))
    h_side = jnp.where(tp == 0, low_h[:, :rank], low_h[:, rank:])
    terms_b = pl.pallas_call(
        functools.partial(terms_b_kernel, n),
        out_shape=jax.ShapeDtypeStruct((n, rank, block_cols), jnp.bfloat16),
        in_specs=[SMEM] * 3 + [ANY, VMEM],
        out_specs=VMEM,
        scratch_shapes=[pltpu.VMEM((rows, block_cols), jnp.bfloat16), pltpu.SemaphoreType.DMA],
        compiler_params=params(),
        cost_estimate=cost(2 * rows * block_cols * n * rank, rows * block_cols * 2),
        name="terms_b",
    )(ids, lengths, slot_job, grad_out, h_side)
    grad_b = chain_scatter(terms_b, f, n)

    scale_rows = jnp.repeat(scales, BLOCK, axis=1)
    result = None
    for c in range(CHUNKS):
        more = [] if result is None else [result]
        result = pl.pallas_call(
            functools.partial(base_kernel, n, c),
            out_shape=jax.ShapeDtypeStruct((rows, width), jnp.bfloat16),
            in_specs=[SMEM] + [VMEM] * 3 + [ANY] * (10 + len(more)),
            out_specs=ANY,
            scratch_shapes=[
                pltpu.VMEM((2, size, wide), jnp.bfloat16),
                pltpu.VMEM((2, size, n * both), jnp.bfloat16),
                pltpu.VMEM((2, rows, size), jnp.bfloat16),
                pltpu.SemaphoreType.DMA((2, n)),
                pltpu.SemaphoreType.DMA((2,)),
                pltpu.SemaphoreType.DMA((2,)),
            ],
            input_output_aliases={14: 0} if more else {},
            compiler_params=params(),
            cost_estimate=cost(2 * rows * 2 * size * (wide + n * both), 2 * size * wide * 2 + rows * wide * 2),
            name="base",
        )(ids, grad_out, masked_u, scale_rows, a_all, codes, *code_blocks[c], *code_swapped[c], *more)
    return result, grad_a[None], grad_b.T[None]


def local_any(activations, grad_out, codes, scales, adapter_a, adapter_b, lengths, slot_job):
    rows = activations.shape[0]
    width = activations.shape[1]
    wide = grad_out.shape[1]
    half = wide // 2
    both = adapter_a.shape[2]
    rank = both // 2
    jobs = lengths.shape[0]
    shards = lax.axis_size(("tp", "dp"))
    column = lax.axis_index(("tp", "dp"))
    block_cols = wide // shards
    first = lax.axis_index("fsdp") * rows
    starts = jnp.cumsum(lengths) - lengths
    positions = first + jnp.arange(rows, dtype=jnp.int32)
    row_job = jnp.sum((positions[:, None] >= starts[None, :]).astype(jnp.int32), axis=1) - 1
    onehot = row_job[:, None] == slot_job[None, :]
    scale_cols = jnp.repeat(jnp.repeat(scales, BLOCK, axis=0), BLOCK, axis=1)
    weight = (lax.all_gather(codes, "fsdp", axis=1, tiled=True).astype(jnp.float32) * scale_cols).astype(jnp.bfloat16)
    frozen = lax.dot_general(grad_out, weight, NT, preferred_element_type=jnp.float32)
    g_block = lax.dynamic_slice_in_dim(grad_out, column * block_cols, block_cols, 1)
    key_side = column * block_cols < half
    a_every = lax.all_gather(adapter_a, "fsdp", axis=0, tiled=True)
    b_every = lax.all_gather(adapter_b, "fsdp", axis=0, tiled=True)
    h_every = jnp.einsum("ri,sic->rsc", activations, a_every, preferred_element_type=jnp.float32)
    u_every = jnp.einsum("ro,sok->rsk", g_block, b_every, preferred_element_type=jnp.float32)
    h_part = jnp.sum(jnp.where(onehot[:, :, None], h_every, 0.0), axis=1)
    u_block = jnp.sum(jnp.where(onehot[:, :, None], u_every, 0.0), axis=1)
    u_part = jnp.concatenate([jnp.where(key_side, u_block, 0.0), jnp.where(key_side, 0.0, u_block)], axis=1)
    low_h = lax.psum(h_part.astype(jnp.bfloat16), ("tp", "dp"))
    low_u = lax.psum(u_part.astype(jnp.bfloat16), ("tp", "dp"))
    masked_u = jnp.where(onehot[:, :, None], low_u[:, None, :], 0).reshape(rows, jobs * both)
    branch = jnp.einsum("rsc,sic->ri", masked_u.reshape(rows, jobs, both), a_every, preferred_element_type=jnp.float32)
    input_gradient = (frozen + adapter_scale * branch).astype(jnp.bfloat16)
    h_side = jnp.where(key_side, low_h[:, :rank], low_h[:, rank:])
    masked_h = jnp.where(onehot[:, :, None], h_side[:, None, :], 0).reshape(rows, jobs * rank)
    down = lax.dot_general(activations, masked_u, TN, preferred_element_type=jnp.float32) * adapter_scale
    up = lax.dot_general(g_block, masked_h, TN, preferred_element_type=jnp.float32) * adapter_scale
    down = down.reshape(width, jobs, both).astype(jnp.bfloat16)
    up = up.reshape(block_cols, jobs, rank).astype(jnp.bfloat16)
    summed_a = lax.psum_scatter(down, "fsdp", scatter_dimension=1, tiled=True).astype(jnp.float32)
    summed_b = lax.psum_scatter(up, "fsdp", scatter_dimension=1, tiled=True).astype(jnp.float32)
    return input_gradient, jnp.transpose(summed_a, (1, 0, 2)), jnp.transpose(summed_b, (1, 0, 2))


def solution(mesh):
    in_specs = (
        P(("groups", "fsdp"), ("tp", "dp")),
        P(("groups", "fsdp"), None),
        P(("tp", "dp"), "fsdp"),
        P(("tp", "dp"), None),
        P("fsdp", ("tp", "dp"), None),
        P("fsdp", ("tp", "dp"), None),
        P("groups"),
        P(),
    )
    out_specs = (
        P(("groups", "fsdp"), ("tp", "dp")),
        P(("groups", "fsdp"), ("tp", "dp"), None),
        P(("groups", "fsdp"), ("tp", "dp"), None),
    )
    shape = dict(mesh.shape)
    chain = shape == {"groups": 2, "fsdp": 4, "tp": 2, "dp": 2}
    local = local_chain if chain else local_any
    return jax.shard_map(local, mesh=mesh, in_specs=in_specs, out_specs=out_specs, check_vma=False)
```

```python
import functools
import math
import jax
import jax.numpy as jnp
from jax import lax
from jax.experimental import pallas as pl
from jax.experimental.pallas import tpu as pltpu
from jax.sharding import PartitionSpec as P

BLOCK = 128
CUTS = (2, 3, 3)
SUM_COST = 20
LATE = True
BASE_COST = 0

adapter_scale = 2.0

SWAP = [(0, 1), (1, 0)]
NT = (((1,), (1,)), ((), ()))
TN = (((0,), (0,)), ((), ()))

HBM = pl.BlockSpec(memory_space=pltpu.HBM)
ANY = pl.BlockSpec(memory_space=pl.ANY)
SMEM = pl.BlockSpec(memory_space=pltpu.SMEM)
VMEM = pl.BlockSpec(memory_space=pltpu.VMEM)
VMEM_LIMIT = 48 * 1024 * 1024


def swap_groups(blocks, f, n):
    others = jnp.stack([lax.dynamic_index_in_dim(blocks, (f + k) % n, 0, keepdims=False) for k in range(1, n)])
    return lax.ppermute(others, "groups", SWAP)


def hold(x, after):
    return pl.pallas_call(
        lambda *refs: None,
        out_shape=jax.ShapeDtypeStruct(x.shape, x.dtype),
        in_specs=[HBM] * (1 + len(after)),
        out_specs=HBM,
        input_output_aliases={0: 0},
        cost_estimate=cost(),
        name="hold",
    )(x, *after)


def pack(a_own, codes, ids, size):
    half, both = a_own.shape[0] // 2, a_own.shape[1]
    parts = codes.shape[1] // both

    def kernel(ids, a_own, codes, out, held, sems):
        first = pl.multiple_of(ids[1] * half, half)
        copies = [pltpu.make_async_copy(a_own.at[pl.ds(first, half)], held.at[pl.ds(0, half)], sems.at[parts])]
        for k in range(parts):
            src = codes.at[pl.ds(first, size), pl.ds(k * both, both)]
            copies.append(pltpu.make_async_copy(src, held.at[pl.ds(half + k * size, size)], sems.at[k]))
        for copy in copies:
            copy.start()
        for copy in copies:
            copy.wait()
        copy = pltpu.make_async_copy(held, out, sems.at[0])
        copy.start()
        copy.wait()

    shape = (half + parts * size, both)
    return pl.pallas_call(
        kernel,
        out_shape=jax.ShapeDtypeStruct(shape, a_own.dtype),
        in_specs=[SMEM, HBM, HBM],
        out_specs=HBM,
        scratch_shapes=[pltpu.VMEM(shape, a_own.dtype), pltpu.SemaphoreType.DMA((parts + 1,))],
        cost_estimate=cost(),
        name="pack",
    )(ids, a_own, codes)


def inward(x):
    return lax.ppermute(x, "fsdp", [(0, 1), (3, 2)])


def inside(x):
    return lax.ppermute(x, "fsdp", [(1, 2), (2, 1)])


def outward(x):
    return lax.ppermute(x, "fsdp", [(1, 0), (2, 3)])


def slot_bounds(slot, lengths, slot_job, first):
    job = slot_job[slot]
    start = jnp.int32(0)
    for j in range(lengths.shape[0]):
        start = start + jnp.where(j < job, lengths[j], 0)
    return start - first, start - first + lengths[job]


def row_mask(slot, lengths, slot_job, first, shape):
    low, high = slot_bounds(slot, lengths, slot_job, first)
    row = lax.broadcasted_iota(jnp.int32, shape, 0)
    return (row >= low) & (row < high)


def u_kernel(n, ids, lengths, slot_job, grad, factors, *refs):
    out, g_all, b_all, sems = refs[-4:]
    f, column = ids[0], ids[2]
    rows, cols = g_all.shape
    rank = out.shape[1]
    grab = pltpu.make_async_copy(grad.at[:, pl.ds(pl.multiple_of(column * cols, cols), cols)], g_all, sems.at[0])
    grab.start()
    fetch = pltpu.make_async_copy(factors, b_all, sems.at[1])
    fetch.start()
    fetch.wait()
    grab.wait()
    total = jnp.zeros(out.shape, jnp.float32)
    for s in range(n):
        part = lax.dot_general(g_all[...], b_all[s], NT, preferred_element_type=jnp.float32)
        total = jnp.where(row_mask(s, lengths, slot_job, f * rows, out.shape), part, total)
    out[...] = total.astype(out.dtype)


def fetch_other(slot, f, n, own, others, dst, sem):
    pl.when(f == slot)(lambda: pltpu.make_async_copy(own, dst, sem).start())
    pl.when(f != slot)(lambda: pltpu.make_async_copy(others.at[lax.rem(slot - f + 2 * n - 1, n)], dst, sem).start())


def h_kernel(n, ids, lengths, slot_job, acts, own, others, first_blocks, *refs):
    out, a_all, sems = refs[-3:]
    f, g = ids[0], ids[1]
    rows = acts.shape[0]
    half = own.shape[0] // 2
    both = out.shape[1]
    here, there = pl.multiple_of(g * half, half), pl.multiple_of((1 - g) * half, half)
    for s in range(n):
        dst = a_all.at[pl.ds(here, half), pl.ds(s * both, both)]
        pltpu.make_async_copy(first_blocks.at[s, pl.ds(0, half)], dst, sems.at[s, 0]).start()
        fetch_other(s, f, n, own.at[pl.ds(there, half)], others, a_all.at[pl.ds(there, half), pl.ds(s * both, both)], sems.at[s, 1])
    for s in range(n):
        for side in range(2):
            pltpu.make_async_copy(own.at[pl.ds(0, half)], a_all.at[pl.ds(0, half), pl.ds(s * both, both)], sems.at[s, side]).wait()
    product = jnp.dot(acts[...], a_all[...], preferred_element_type=jnp.float32)
    total = jnp.zeros(out.shape, jnp.float32)
    for s in range(n):
        total = jnp.where(row_mask(s, lengths, slot_job, f * rows, out.shape), product[:, s * both:(s + 1) * both], total)
    out[...] = total.astype(out.dtype)


def added(parts):
    total = parts[0].astype(jnp.float32)
    for part in parts[1:]:
        total = total + part.astype(jnp.float32)
    return total.astype(jnp.bfloat16)


def terms_a_kernel(n, ids, lengths, slot_job, acts, u_parts, masked, *refs):
    outs, (held, sems) = refs[:n], refs[n:]
    f = ids[0]
    shards, rows, _ = u_parts.shape
    both = held.shape[2]
    key = added([u_parts[k] for k in range(shards // 2)])
    value = added([u_parts[k] for k in range(shards // 2, shards)])
    doubled = jnp.concatenate([key, value], axis=1).astype(jnp.float32) * adapter_scale
    for s in range(n):
        part = jnp.where(row_mask(s, lengths, slot_job, f * rows, doubled.shape), doubled, 0.0).astype(jnp.bfloat16)
        masked[:, s * both:(s + 1) * both] = part
    left = f < n // 2
    third = jnp.where(f == 0, 1, jnp.where(f == n - 1, n - 2, jnp.where(left, 0, n - 1)))
    copies = [pltpu.make_async_copy(held.at[k], outs[k], sems.at[k]) for k in range(n)]
    for k, s in enumerate((jnp.where(left, n - 1, 0), jnp.where(left, n - 2, 1), third, f)):
        part = jnp.where(row_mask(s, lengths, slot_job, f * rows, doubled.shape), doubled, 0.0).astype(jnp.bfloat16)
        held[k] = lax.dot_general(acts[...], part, TN, preferred_element_type=jnp.float32).astype(jnp.bfloat16)
        copies[k].start()
    for copy in copies:
        copy.wait()


def terms_b_kernel(n, ids, lengths, slot_job, grad, h_parts, out, g_all, sem):
    f, column = ids[0], ids[2]
    rows, cols = g_all.shape
    shards = h_parts.shape[0]
    rank = out.shape[1]
    grab = pltpu.make_async_copy(grad.at[:, pl.ds(pl.multiple_of(column * cols, cols), cols)], g_all, sem)
    grab.start()
    low_h = added([h_parts[k] for k in range(shards)]).astype(jnp.float32) * adapter_scale
    side = jnp.where(column < shards // 2, low_h[:, :rank], low_h[:, rank:])
    grab.wait()
    for s in range(n):
        part = jnp.where(row_mask(s, lengths, slot_job, f * rows, side.shape), side, 0.0).astype(jnp.bfloat16)
        out[s] = lax.dot_general(part, g_all[...], TN, preferred_element_type=jnp.float32).astype(jnp.bfloat16)


def base_kernel(n, offset, size, packed, ids, grad, far_core, far_other, masked, far_masked, scale_rows, first_blocks, blocks, *refs):
    out, far_out, grads, masks, codes, factors, result, sems, in_sems, out_sem = refs[-10:]
    g, dp = ids[1], ids[3]
    rows, wide = grad.shape
    half, both, cols = out.shape[1] // 2, first_blocks.shape[2], wide // n
    part = far_core.shape[0]
    first = pl.multiple_of(g * half + offset, BLOCK)
    copies = [
        pltpu.make_async_copy(grad, grads.at[pl.ds(0, rows)], in_sems.at[0]),
        pltpu.make_async_copy(far_core, grads.at[pl.ds(pl.multiple_of(rows + dp * part, part), part)], in_sems.at[1]),
        pltpu.make_async_copy(far_other, grads.at[pl.ds(pl.multiple_of(rows + (1 - dp) * part, part), part)], in_sems.at[2]),
        pltpu.make_async_copy(masked, masks.at[pl.ds(0, rows)], in_sems.at[3]),
        pltpu.make_async_copy(far_masked, masks.at[pl.ds(rows, rows)], in_sems.at[4]),
    ]
    for s in range(n):
        if packed:
            for k in range(cols // both):
                src = first_blocks.at[s, pl.ds(half + k * size, size)]
                copies.append(pltpu.make_async_copy(src, codes.at[:, pl.ds(s * cols + k * both, both)], sems.at[s, k]))
        else:
            copies.append(pltpu.make_async_copy(blocks.at[s], codes.at[:, pl.ds(s * cols, cols)], sems.at[s, 0]))
        copies.append(pltpu.make_async_copy(first_blocks.at[s, pl.ds(offset, size)], factors.at[:, pl.ds(s * both, both)], sems.at[n, s]))
    for copy in copies:
        copy.start()
    for copy in copies:
        copy.wait()
    weight = []
    for b in range(size // BLOCK):
        scale = scale_rows[pl.ds(first // BLOCK + b, 1), :]
        weight.append((codes[b * BLOCK:(b + 1) * BLOCK, :].astype(jnp.float32) * scale).astype(jnp.bfloat16))
    weight = jnp.concatenate(weight, axis=0)
    for side in range(2):
        take = slice(side * rows, (side + 1) * rows)
        total = lax.dot_general(grads[take], weight, NT, preferred_element_type=jnp.float32)
        total += lax.dot_general(masks[take], factors[...], NT, preferred_element_type=jnp.float32)
        if side == 0:
            result[...] = total.astype(jnp.bfloat16)
            keep = pltpu.make_async_copy(result, out.at[:, pl.ds(first, size)], out_sem)
            keep.start()
        else:
            far_out[...] = total.astype(jnp.bfloat16)
    keep.wait()


def params():
    return pltpu.CompilerParams(vmem_limit_bytes=VMEM_LIMIT)


def cost(us=0):
    return pl.CostEstimate(flops=int(us * 1.1e9) + 1, bytes_accessed=1, transcendentals=0)


def sum_terms(own, *arrived):
    def kernel(own, *refs):
        total = own[...].astype(jnp.float32)
        for ref in refs[:-1]:
            total = total + ref[...].astype(jnp.float32)
        refs[-1][...] = total

    return pl.pallas_call(
        kernel,
        out_shape=jax.ShapeDtypeStruct(own.shape, jnp.float32),
        compiler_params=params(),
        cost_estimate=cost(SUM_COST),
        name="sum_terms",
    )(own, *arrived)


def piece_of(whole, ids, offset, size, after):
    half = whole.shape[0] // 2
    step = math.gcd(math.gcd(offset, size), half)

    def kernel(ids, whole, *refs):
        refs[-1][...] = whole[...]

    return pl.pallas_call(
        kernel,
        out_shape=jax.ShapeDtypeStruct((size, whole.shape[1]), whole.dtype),
        grid_spec=pltpu.PrefetchScalarGridSpec(
            num_scalar_prefetch=1,
            grid=(size // step,),
            in_specs=[pl.BlockSpec((step, whole.shape[1]), lambda i, ids: ((ids[1] * half + offset) // step + i, 0))] + [HBM] * len(after),
            out_specs=pl.BlockSpec((step, whole.shape[1]), lambda i, ids: (i, 0)),
        ),
        cost_estimate=cost(),
        name="piece",
    )(ids, whole, *after)


def place(whole, part, ids, offset):
    def kernel(ids, part, _, out, sem):
        first = pl.multiple_of((1 - ids[1]) * (out.shape[1] // 2) + offset, BLOCK)
        copy = pltpu.make_async_copy(part, out.at[:, pl.ds(first, part.shape[1])], sem)
        copy.start()
        copy.wait()

    return pl.pallas_call(
        kernel,
        out_shape=jax.ShapeDtypeStruct(whole.shape, whole.dtype),
        in_specs=[SMEM, VMEM, HBM],
        out_specs=HBM,
        scratch_shapes=[pltpu.SemaphoreType.DMA],
        input_output_aliases={2: 0},
        compiler_params=params(),
        cost_estimate=cost(),
        name="place",
    )(ids, part, whole)


def local_chain(activations, grad_out, codes, scales, adapter_a, adapter_b, lengths, slot_job):
    n = 4
    rows, width = activations.shape
    wide = grad_out.shape[1]
    both = adapter_a.shape[2]
    rank = both // 2
    cols = codes.shape[1]
    block_cols = adapter_b.shape[1]
    half = width // 2
    f, g = lax.axis_index("fsdp"), lax.axis_index("groups")
    tp, dp = lax.axis_index("tp"), lax.axis_index("dp")
    ids = jnp.stack([f, g, tp * 2 + dp, dp]).astype(jnp.int32)
    a_own = adapter_a[0]
    shards = ("tp", "dp")

    b_all = lax.all_gather(adapter_b[0].T, "fsdp")
    part = rows // 2
    far_core = lax.ppermute(lax.dynamic_slice_in_dim(grad_out, dp * part, part, 0), "groups", SWAP)
    far_other = lax.ppermute(far_core, "dp", SWAP)

    sizes = [half * parts // sum(CUTS) for parts in CUTS]
    offsets = [sum(sizes[:c]) for c in range(len(CUTS))]
    first_blocks = lax.all_gather(pack(a_own, codes, ids, sizes[0]), "fsdp")
    code_blocks = [first_blocks] + [
        lax.all_gather(lax.dynamic_slice_in_dim(codes, g * half + offset, size, 0), "fsdp") for offset, size in zip(offsets[1:], sizes[1:])
    ]

    u_part = pl.pallas_call(
        functools.partial(u_kernel, n),
        out_shape=jax.ShapeDtypeStruct((rows, rank), jnp.bfloat16),
        in_specs=[SMEM] * 3 + [HBM] * 2,
        out_specs=VMEM,
        scratch_shapes=[
            pltpu.VMEM((rows, block_cols), jnp.bfloat16),
            pltpu.VMEM((n, rank, block_cols), jnp.bfloat16),
            pltpu.SemaphoreType.DMA((2,)),
        ],
        compiler_params=params(),
        cost_estimate=cost(),
        name="low_u",
    )(ids, lengths, slot_job, grad_out, b_all)
    masked_u, far, middle, last, own_a = pl.pallas_call(
        functools.partial(terms_a_kernel, n),
        out_shape=(jax.ShapeDtypeStruct((rows, n * both), jnp.bfloat16),) + (jax.ShapeDtypeStruct((width, both), jnp.bfloat16),) * 4,
        in_specs=[SMEM] * 3 + [VMEM] * 2,
        out_specs=(VMEM,) + (HBM,) * 4,
        scratch_shapes=[pltpu.VMEM((n, width, both), jnp.bfloat16), pltpu.SemaphoreType.DMA((n,))],
        compiler_params=params(),
        cost_estimate=cost(),
        name="terms_a",
    )(ids, lengths, slot_job, activations, lax.all_gather(u_part, shards))
    far_in, middle_in, near = inward(far), inward(middle), inward(last)
    far_masked = lax.ppermute(masked_u, "groups", SWAP)
    a_others = swap_groups(first_blocks[:, :half], f, n)
    far = inside(far + far_in)

    scale_rows = jnp.repeat(scales, BLOCK, axis=1)

    def base(c, before, after):
        blocks, offset, size = code_blocks[c], offsets[c], sizes[c]
        more = [] if before is None else [before]
        return pl.pallas_call(
            functools.partial(base_kernel, n, offset, size, c == 0),
            out_shape=(jax.ShapeDtypeStruct((rows, width), jnp.bfloat16), jax.ShapeDtypeStruct((rows, size), jnp.bfloat16)),
            in_specs=[SMEM] + [ANY] * 5 + [VMEM] + [HBM] * (2 + len(more)) + [ANY] * len(after),
            out_specs=(HBM, VMEM),
            scratch_shapes=[
                pltpu.VMEM((2 * rows, wide), jnp.bfloat16),
                pltpu.VMEM((2 * rows, n * both), jnp.bfloat16),
                pltpu.VMEM((size, wide), jnp.bfloat16),
                pltpu.VMEM((size, n * both), jnp.bfloat16),
                pltpu.VMEM((rows, size), jnp.bfloat16),
                pltpu.SemaphoreType.DMA((n + 1, wide // n // both)),
                pltpu.SemaphoreType.DMA((5,)),
                pltpu.SemaphoreType.DMA,
            ],
            input_output_aliases={9: 0} if more else {},
            compiler_params=params(),
            cost_estimate=cost(BASE_COST),
            name="base",
        )(ids, grad_out, far_core, far_other, masked_u, far_masked, scale_rows, first_blocks, blocks, *more, *after)

    h_part = pl.pallas_call(
        functools.partial(h_kernel, n),
        out_shape=jax.ShapeDtypeStruct((rows, both), jnp.bfloat16),
        in_specs=[SMEM] * 3 + [VMEM] + [ANY] * 3,
        out_specs=VMEM,
        scratch_shapes=[pltpu.VMEM((width, n * both), jnp.bfloat16), pltpu.SemaphoreType.DMA((n, 2))],
        compiler_params=params(),
        cost_estimate=cost(),
        name="low_h",
    )(ids, lengths, slot_job, activations, a_own, a_others, first_blocks)
    terms_b = pl.pallas_call(
        functools.partial(terms_b_kernel, n),
        out_shape=jax.ShapeDtypeStruct((n, rank, block_cols), jnp.bfloat16),
        in_specs=[SMEM] * 3 + [HBM, VMEM],
        out_specs=VMEM,
        scratch_shapes=[pltpu.VMEM((rows, block_cols), jnp.bfloat16), pltpu.SemaphoreType.DMA],
        compiler_params=params(),
        cost_estimate=cost(),
        name="terms_b",
    )(ids, lengths, slot_job, grad_out, lax.all_gather(h_part, shards))
    grad_b = lax.psum_scatter(terms_b, "fsdp", scatter_dimension=0).astype(jnp.float32)
    middle = inside(middle + middle_in)

    result, far_out = base(0, None, ())
    parts = [lax.ppermute(far_out, "groups", SWAP)]
    last_out = last + far
    for c in range(1, len(CUTS)):
        result, far_out = base(c, result, (last_out,) if c == len(CUTS) - 1 and LATE else (terms_b,))
        parts.append(lax.ppermute(far_out, "groups", SWAP))
    for part, offset in zip(parts, offsets):
        result = place(result, part, ids, offset)
    grad_a = sum_terms(own_a, near, middle, outward(last_out))
    return result, grad_a[None], grad_b.T[None]


def local_any(activations, grad_out, codes, scales, adapter_a, adapter_b, lengths, slot_job):
    rows = activations.shape[0]
    width = activations.shape[1]
    wide = grad_out.shape[1]
    half = wide // 2
    both = adapter_a.shape[2]
    rank = both // 2
    jobs = lengths.shape[0]
    shards = lax.axis_size(("tp", "dp"))
    column = lax.axis_index(("tp", "dp"))
    block_cols = wide // shards
    first = lax.axis_index("fsdp") * rows
    starts = jnp.cumsum(lengths) - lengths
    positions = first + jnp.arange(rows, dtype=jnp.int32)
    row_job = jnp.sum((positions[:, None] >= starts[None, :]).astype(jnp.int32), axis=1) - 1
    onehot = row_job[:, None] == slot_job[None, :]
    scale_cols = jnp.repeat(jnp.repeat(scales, BLOCK, axis=0), BLOCK, axis=1)
    weight = (lax.all_gather(codes, "fsdp", axis=1, tiled=True).astype(jnp.float32) * scale_cols).astype(jnp.bfloat16)
    frozen = lax.dot_general(grad_out, weight, NT, preferred_element_type=jnp.float32)
    g_block = lax.dynamic_slice_in_dim(grad_out, column * block_cols, block_cols, 1)
    key_side = column * block_cols < half
    a_every = lax.all_gather(adapter_a, "fsdp", axis=0, tiled=True)
    b_every = lax.all_gather(adapter_b, "fsdp", axis=0, tiled=True)
    h_every = jnp.einsum("ri,sic->rsc", activations, a_every, preferred_element_type=jnp.float32)
    u_every = jnp.einsum("ro,sok->rsk", g_block, b_every, preferred_element_type=jnp.float32)
    h_part = jnp.sum(jnp.where(onehot[:, :, None], h_every, 0.0), axis=1)
    u_block = jnp.sum(jnp.where(onehot[:, :, None], u_every, 0.0), axis=1)
    u_part = jnp.concatenate([jnp.where(key_side, u_block, 0.0), jnp.where(key_side, 0.0, u_block)], axis=1)
    low_h = lax.psum(h_part.astype(jnp.bfloat16), ("tp", "dp"))
    low_u = lax.psum(u_part.astype(jnp.bfloat16), ("tp", "dp"))
    masked_u = jnp.where(onehot[:, :, None], low_u[:, None, :], 0).reshape(rows, jobs * both)
    branch = jnp.einsum("rsc,sic->ri", masked_u.reshape(rows, jobs, both), a_every, preferred_element_type=jnp.float32)
    input_gradient = (frozen + adapter_scale * branch).astype(jnp.bfloat16)
    h_side = jnp.where(key_side, low_h[:, :rank], low_h[:, rank:])
    masked_h = jnp.where(onehot[:, :, None], h_side[:, None, :], 0).reshape(rows, jobs * rank)
    down = lax.dot_general(activations, masked_u, TN, preferred_element_type=jnp.float32) * adapter_scale
    up = lax.dot_general(g_block, masked_h, TN, preferred_element_type=jnp.float32) * adapter_scale
    down = down.reshape(width, jobs, both).astype(jnp.bfloat16)
    up = up.reshape(block_cols, jobs, rank).astype(jnp.bfloat16)
    summed_a = lax.psum_scatter(down, "fsdp", scatter_dimension=1, tiled=True).astype(jnp.float32)
    summed_b = lax.psum_scatter(up, "fsdp", scatter_dimension=1, tiled=True).astype(jnp.float32)
    return input_gradient, jnp.transpose(summed_a, (1, 0, 2)), jnp.transpose(summed_b, (1, 0, 2))


def solution(mesh):
    in_specs = (
        P(("groups", "fsdp"), ("tp", "dp")),
        P(("groups", "fsdp"), None),
        P(("tp", "dp"), "fsdp"),
        P(("tp", "dp"), None),
        P("fsdp", ("tp", "dp"), None),
        P("fsdp", ("tp", "dp"), None),
        P("groups"),
        P(),
    )
    out_specs = (
        P(("groups", "fsdp"), ("tp", "dp")),
        P(("groups", "fsdp"), ("tp", "dp"), None),
        P(("groups", "fsdp"), ("tp", "dp"), None),
    )
    shape = dict(mesh.shape)
    chain = shape == {"groups": 2, "fsdp": 4, "tp": 2, "dp": 2}
    local = local_chain if chain else local_any
    return jax.shard_map(local, mesh=mesh, in_specs=in_specs, out_specs=out_specs, check_vma=False)
```

```python
import functools
import math
import jax
import jax.numpy as jnp
from jax import lax
from jax.experimental import pallas as pl
from jax.experimental.pallas import tpu as pltpu
from jax.sharding import PartitionSpec as P

BLOCK = 128
CUTS = (2, 3, 3)
SUM_COST = 20
LATE = True
BASE_COST = 0

adapter_scale = 2.0

SWAP = [(0, 1), (1, 0)]
NT = (((1,), (1,)), ((), ()))
TN = (((0,), (0,)), ((), ()))

HBM = pl.BlockSpec(memory_space=pltpu.HBM)
ANY = pl.BlockSpec(memory_space=pl.ANY)
SMEM = pl.BlockSpec(memory_space=pltpu.SMEM)
VMEM = pl.BlockSpec(memory_space=pltpu.VMEM)
VMEM_LIMIT = 48 * 1024 * 1024


def swap_groups(blocks, f, n):
    others = jnp.stack([lax.dynamic_index_in_dim(blocks, (f + k) % n, 0, keepdims=False) for k in range(1, n)])
    return lax.ppermute(others, "groups", SWAP)


def hold(x, after):
    return pl.pallas_call(
        lambda *refs: None,
        out_shape=jax.ShapeDtypeStruct(x.shape, x.dtype),
        in_specs=[HBM] * (1 + len(after)),
        out_specs=HBM,
        input_output_aliases={0: 0},
        cost_estimate=cost(),
        name="hold",
    )(x, *after)


def pack(a_own, codes, ids, size):
    half, both = a_own.shape[0] // 2, a_own.shape[1]
    parts = codes.shape[1] // both

    def kernel(ids, a_own, codes, out, held, sems, out_sems):
        first = pl.multiple_of(ids[1] * half, half)
        copies = [pltpu.make_async_copy(a_own.at[pl.ds(first, half)], held.at[pl.ds(0, half)], sems.at[parts])]
        for k in range(parts):
            src = codes.at[pl.ds(first, size), pl.ds(k * both, both)]
            copies.append(pltpu.make_async_copy(src, held.at[pl.ds(half + k * size, size)], sems.at[k]))
        places = [pl.ds(half + k * size, size) for k in range(parts)]
        places = [pl.ds(0, half)] + places
        stores = [pltpu.make_async_copy(held.at[place], out.at[place], out_sems.at[k]) for k, place in enumerate(places)]
        for copy in copies:
            copy.start()
        for copy, store in zip(copies, stores):
            copy.wait()
            store.start()
        for store in stores:
            store.wait()

    shape = (half + parts * size, both)
    return pl.pallas_call(
        kernel,
        out_shape=jax.ShapeDtypeStruct(shape, a_own.dtype),
        in_specs=[SMEM, HBM, HBM],
        out_specs=HBM,
        scratch_shapes=[pltpu.VMEM(shape, a_own.dtype), pltpu.SemaphoreType.DMA((parts + 1,)), pltpu.SemaphoreType.DMA((parts + 1,))],
        cost_estimate=cost(),
        name="pack",
    )(ids, a_own, codes)


def inward(x):
    return lax.ppermute(x, "fsdp", [(0, 1), (3, 2)])


def inside(x):
    return lax.ppermute(x, "fsdp", [(1, 2), (2, 1)])


def outward(x):
    return lax.ppermute(x, "fsdp", [(1, 0), (2, 3)])


def slot_bounds(slot, lengths, slot_job, first):
    job = slot_job[slot]
    start = jnp.int32(0)
    for j in range(lengths.shape[0]):
        start = start + jnp.where(j < job, lengths[j], 0)
    return start - first, start - first + lengths[job]


def row_mask(slot, lengths, slot_job, first, shape):
    low, high = slot_bounds(slot, lengths, slot_job, first)
    row = lax.broadcasted_iota(jnp.int32, shape, 0)
    return (row >= low) & (row < high)


def u_kernel(n, ids, lengths, slot_job, grad, factors, *refs):
    out, g_all, b_all, sems = refs[-4:]
    f, column = ids[0], ids[2]
    rows, cols = g_all.shape
    rank = out.shape[1]
    grab = pltpu.make_async_copy(grad.at[:, pl.ds(pl.multiple_of(column * cols, cols), cols)], g_all, sems.at[0])
    grab.start()
    fetch = pltpu.make_async_copy(factors, b_all, sems.at[1])
    fetch.start()
    fetch.wait()
    grab.wait()
    total = jnp.zeros(out.shape, jnp.float32)
    for s in range(n):
        part = lax.dot_general(g_all[...], b_all[s], NT, preferred_element_type=jnp.float32)
        total = jnp.where(row_mask(s, lengths, slot_job, f * rows, out.shape), part, total)
    out[...] = total.astype(out.dtype)


def fetch_other(slot, f, n, own, others, dst, sem):
    pl.when(f == slot)(lambda: pltpu.make_async_copy(own, dst, sem).start())
    pl.when(f != slot)(lambda: pltpu.make_async_copy(others.at[lax.rem(slot - f + 2 * n - 1, n)], dst, sem).start())


def h_kernel(n, ids, lengths, slot_job, acts, own, others, first_blocks, *refs):
    out, a_all, sems = refs[-3:]
    f, g = ids[0], ids[1]
    rows = acts.shape[0]
    half = own.shape[0] // 2
    both = out.shape[1]
    here, there = pl.multiple_of(g * half, half), pl.multiple_of((1 - g) * half, half)
    for s in range(n):
        dst = a_all.at[pl.ds(here, half), pl.ds(s * both, both)]
        pltpu.make_async_copy(first_blocks.at[s, pl.ds(0, half)], dst, sems.at[s, 0]).start()
        fetch_other(s, f, n, own.at[pl.ds(there, half)], others, a_all.at[pl.ds(there, half), pl.ds(s * both, both)], sems.at[s, 1])
    for s in range(n):
        for side in range(2):
            pltpu.make_async_copy(own.at[pl.ds(0, half)], a_all.at[pl.ds(0, half), pl.ds(s * both, both)], sems.at[s, side]).wait()
    product = jnp.dot(acts[...], a_all[...], preferred_element_type=jnp.float32)
    total = jnp.zeros(out.shape, jnp.float32)
    for s in range(n):
        total = jnp.where(row_mask(s, lengths, slot_job, f * rows, out.shape), product[:, s * both:(s + 1) * both], total)
    out[...] = total.astype(out.dtype)


def added(parts):
    total = parts[0].astype(jnp.float32)
    for part in parts[1:]:
        total = total + part.astype(jnp.float32)
    return total.astype(jnp.bfloat16)


def terms_a_kernel(n, ids, lengths, slot_job, acts, u_parts, masked, *refs):
    outs, (held, sems) = refs[:n], refs[n:]
    f = ids[0]
    shards, rows, _ = u_parts.shape
    both = held.shape[2]
    key = added([u_parts[k] for k in range(shards // 2)])
    value = added([u_parts[k] for k in range(shards // 2, shards)])
    doubled = jnp.concatenate([key, value], axis=1).astype(jnp.float32) * adapter_scale
    for s in range(n):
        part = jnp.where(row_mask(s, lengths, slot_job, f * rows, doubled.shape), doubled, 0.0).astype(jnp.bfloat16)
        masked[:, s * both:(s + 1) * both] = part
    left = f < n // 2
    third = jnp.where(f == 0, 1, jnp.where(f == n - 1, n - 2, jnp.where(left, 0, n - 1)))
    copies = [pltpu.make_async_copy(held.at[k], outs[k], sems.at[k]) for k in range(n)]
    for k, s in enumerate((jnp.where(left, n - 1, 0), jnp.where(left, n - 2, 1), third, f)):
        part = jnp.where(row_mask(s, lengths, slot_job, f * rows, doubled.shape), doubled, 0.0).astype(jnp.bfloat16)
        held[k] = lax.dot_general(acts[...], part, TN, preferred_element_type=jnp.float32).astype(jnp.bfloat16)
        copies[k].start()
    for copy in copies:
        copy.wait()


def terms_b_kernel(n, ids, lengths, slot_job, grad, h_parts, out, g_all, sem):
    f, column = ids[0], ids[2]
    rows, cols = g_all.shape
    shards = h_parts.shape[0]
    rank = out.shape[1]
    grab = pltpu.make_async_copy(grad.at[:, pl.ds(pl.multiple_of(column * cols, cols), cols)], g_all, sem)
    grab.start()
    low_h = added([h_parts[k] for k in range(shards)]).astype(jnp.float32) * adapter_scale
    side = jnp.where(column < shards // 2, low_h[:, :rank], low_h[:, rank:])
    grab.wait()
    for s in range(n):
        part = jnp.where(row_mask(s, lengths, slot_job, f * rows, side.shape), side, 0.0).astype(jnp.bfloat16)
        out[s] = lax.dot_general(part, g_all[...], TN, preferred_element_type=jnp.float32).astype(jnp.bfloat16)


def base_kernel(n, offset, size, packed, ids, grad, far_core, far_other, masked, far_masked, scale_rows, first_blocks, blocks, *refs):
    out, far_out, grads, masks, codes, factors, result, sems, in_sems, out_sem = refs[-10:]
    g, dp = ids[1], ids[3]
    rows, wide = grad.shape
    half, both, cols = out.shape[1] // 2, first_blocks.shape[2], wide // n
    part = far_core.shape[0]
    first = pl.multiple_of(g * half + offset, BLOCK)
    near = [
        pltpu.make_async_copy(grad, grads.at[pl.ds(0, rows)], in_sems.at[0]),
        pltpu.make_async_copy(masked, masks.at[pl.ds(0, rows)], in_sems.at[3]),
    ]
    far = [
        pltpu.make_async_copy(far_core, grads.at[pl.ds(pl.multiple_of(rows + dp * part, part), part)], in_sems.at[1]),
        pltpu.make_async_copy(far_other, grads.at[pl.ds(pl.multiple_of(rows + (1 - dp) * part, part), part)], in_sems.at[2]),
        pltpu.make_async_copy(far_masked, masks.at[pl.ds(rows, rows)], in_sems.at[4]),
    ]
    arriving = []
    for s in range(n):
        if packed:
            for k in range(cols // both):
                src = first_blocks.at[s, pl.ds(half + k * size, size)]
                arriving.append(pltpu.make_async_copy(src, codes.at[:, pl.ds(s * cols + k * both, both)], sems.at[s, k]))
        else:
            arriving.append(pltpu.make_async_copy(blocks.at[s], codes.at[:, pl.ds(s * cols, cols)], sems.at[s, 0]))
        near.append(pltpu.make_async_copy(first_blocks.at[s, pl.ds(offset, size)], factors.at[:, pl.ds(s * both, both)], sems.at[n, s]))
    for copy in arriving + near + far:
        copy.start()
    for copy in arriving:
        copy.wait()
    weight = []
    for b in range(size // BLOCK):
        scale = scale_rows[pl.ds(first // BLOCK + b, 1), :]
        weight.append((codes[b * BLOCK:(b + 1) * BLOCK, :].astype(jnp.float32) * scale).astype(jnp.bfloat16))
    weight = jnp.concatenate(weight, axis=0)

    def product(take):
        total = lax.dot_general(grads[take], weight, NT, preferred_element_type=jnp.float32)
        total += lax.dot_general(masks[take], factors[...], NT, preferred_element_type=jnp.float32)
        return total.astype(jnp.bfloat16)

    for copy in near:
        copy.wait()
    result[...] = product(slice(0, rows))
    keep = pltpu.make_async_copy(result, out.at[:, pl.ds(first, size)], out_sem)
    keep.start()
    for copy in far:
        copy.wait()
    far_out[...] = product(slice(rows, 2 * rows))
    keep.wait()


def params():
    return pltpu.CompilerParams(vmem_limit_bytes=VMEM_LIMIT)


def cost(us=0):
    return pl.CostEstimate(flops=int(us * 1.1e9) + 1, bytes_accessed=1, transcendentals=0)


def sum_terms(own, *arrived):
    def kernel(own, *refs):
        total = own[...].astype(jnp.float32)
        for ref in refs[:-1]:
            total = total + ref[...].astype(jnp.float32)
        refs[-1][...] = total

    return pl.pallas_call(
        kernel,
        out_shape=jax.ShapeDtypeStruct(own.shape, jnp.float32),
        compiler_params=params(),
        cost_estimate=cost(SUM_COST),
        name="sum_terms",
    )(own, *arrived)


def piece_of(whole, ids, offset, size, after):
    half = whole.shape[0] // 2
    step = math.gcd(math.gcd(offset, size), half)

    def kernel(ids, whole, *refs):
        refs[-1][...] = whole[...]

    return pl.pallas_call(
        kernel,
        out_shape=jax.ShapeDtypeStruct((size, whole.shape[1]), whole.dtype),
        grid_spec=pltpu.PrefetchScalarGridSpec(
            num_scalar_prefetch=1,
            grid=(size // step,),
            in_specs=[pl.BlockSpec((step, whole.shape[1]), lambda i, ids: ((ids[1] * half + offset) // step + i, 0))] + [HBM] * len(after),
            out_specs=pl.BlockSpec((step, whole.shape[1]), lambda i, ids: (i, 0)),
        ),
        cost_estimate=cost(),
        name="piece",
    )(ids, whole, *after)


def place(whole, part, ids, offset):
    def kernel(ids, part, _, out, sem):
        first = pl.multiple_of((1 - ids[1]) * (out.shape[1] // 2) + offset, BLOCK)
        copy = pltpu.make_async_copy(part, out.at[:, pl.ds(first, part.shape[1])], sem)
        copy.start()
        copy.wait()

    return pl.pallas_call(
        kernel,
        out_shape=jax.ShapeDtypeStruct(whole.shape, whole.dtype),
        in_specs=[SMEM, VMEM, HBM],
        out_specs=HBM,
        scratch_shapes=[pltpu.SemaphoreType.DMA],
        input_output_aliases={2: 0},
        compiler_params=params(),
        cost_estimate=cost(),
        name="place",
    )(ids, part, whole)


def local_chain(activations, grad_out, codes, scales, adapter_a, adapter_b, lengths, slot_job):
    n = 4
    rows, width = activations.shape
    wide = grad_out.shape[1]
    both = adapter_a.shape[2]
    rank = both // 2
    cols = codes.shape[1]
    block_cols = adapter_b.shape[1]
    half = width // 2
    f, g = lax.axis_index("fsdp"), lax.axis_index("groups")
    tp, dp = lax.axis_index("tp"), lax.axis_index("dp")
    ids = jnp.stack([f, g, tp * 2 + dp, dp]).astype(jnp.int32)
    a_own = adapter_a[0]
    shards = ("tp", "dp")

    b_all = lax.all_gather(adapter_b[0].T, "fsdp")
    part = rows // 2
    far_core = lax.ppermute(lax.dynamic_slice_in_dim(grad_out, dp * part, part, 0), "groups", SWAP)
    far_other = lax.ppermute(far_core, "dp", SWAP)

    sizes = [half * parts // sum(CUTS) for parts in CUTS]
    offsets = [sum(sizes[:c]) for c in range(len(CUTS))]
    first_blocks = lax.all_gather(pack(a_own, codes, ids, sizes[0]), "fsdp")
    code_blocks = [first_blocks] + [
        lax.all_gather(lax.dynamic_slice_in_dim(codes, g * half + offset, size, 0), "fsdp") for offset, size in zip(offsets[1:], sizes[1:])
    ]

    u_part = pl.pallas_call(
        functools.partial(u_kernel, n),
        out_shape=jax.ShapeDtypeStruct((rows, rank), jnp.bfloat16),
        in_specs=[SMEM] * 3 + [HBM] * 2,
        out_specs=VMEM,
        scratch_shapes=[
            pltpu.VMEM((rows, block_cols), jnp.bfloat16),
            pltpu.VMEM((n, rank, block_cols), jnp.bfloat16),
            pltpu.SemaphoreType.DMA((2,)),
        ],
        compiler_params=params(),
        cost_estimate=cost(),
        name="low_u",
    )(ids, lengths, slot_job, grad_out, b_all)
    masked_u, far, middle, last, own_a = pl.pallas_call(
        functools.partial(terms_a_kernel, n),
        out_shape=(jax.ShapeDtypeStruct((rows, n * both), jnp.bfloat16),) + (jax.ShapeDtypeStruct((width, both), jnp.bfloat16),) * 4,
        in_specs=[SMEM] * 3 + [VMEM] * 2,
        out_specs=(VMEM,) + (HBM,) * 4,
        scratch_shapes=[pltpu.VMEM((n, width, both), jnp.bfloat16), pltpu.SemaphoreType.DMA((n,))],
        compiler_params=params(),
        cost_estimate=cost(),
        name="terms_a",
    )(ids, lengths, slot_job, activations, lax.all_gather(u_part, shards))
    far_in, middle_in, near = inward(far), inward(middle), inward(last)
    far_masked = lax.ppermute(masked_u, "groups", SWAP)
    a_others = swap_groups(first_blocks[:, :half], f, n)
    far = inside(far + far_in)

    scale_rows = jnp.repeat(scales, BLOCK, axis=1)

    def base(c, before, after):
        blocks, offset, size = code_blocks[c], offsets[c], sizes[c]
        more = [] if before is None else [before]
        return pl.pallas_call(
            functools.partial(base_kernel, n, offset, size, c == 0),
            out_shape=(jax.ShapeDtypeStruct((rows, width), jnp.bfloat16), jax.ShapeDtypeStruct((rows, size), jnp.bfloat16)),
            in_specs=[SMEM] + [ANY] * 5 + [VMEM] + [HBM] * (2 + len(more)) + [ANY] * len(after),
            out_specs=(HBM, VMEM),
            scratch_shapes=[
                pltpu.VMEM((2 * rows, wide), jnp.bfloat16),
                pltpu.VMEM((2 * rows, n * both), jnp.bfloat16),
                pltpu.VMEM((size, wide), jnp.bfloat16),
                pltpu.VMEM((size, n * both), jnp.bfloat16),
                pltpu.VMEM((rows, size), jnp.bfloat16),
                pltpu.SemaphoreType.DMA((n + 1, wide // n // both)),
                pltpu.SemaphoreType.DMA((5,)),
                pltpu.SemaphoreType.DMA,
            ],
            input_output_aliases={9: 0} if more else {},
            compiler_params=params(),
            cost_estimate=cost(BASE_COST),
            name="base",
        )(ids, grad_out, far_core, far_other, masked_u, far_masked, scale_rows, first_blocks, blocks, *more, *after)

    h_part = pl.pallas_call(
        functools.partial(h_kernel, n),
        out_shape=jax.ShapeDtypeStruct((rows, both), jnp.bfloat16),
        in_specs=[SMEM] * 3 + [VMEM] + [ANY] * 3,
        out_specs=VMEM,
        scratch_shapes=[pltpu.VMEM((width, n * both), jnp.bfloat16), pltpu.SemaphoreType.DMA((n, 2))],
        compiler_params=params(),
        cost_estimate=cost(),
        name="low_h",
    )(ids, lengths, slot_job, activations, a_own, a_others, first_blocks)
    terms_b = pl.pallas_call(
        functools.partial(terms_b_kernel, n),
        out_shape=jax.ShapeDtypeStruct((n, rank, block_cols), jnp.bfloat16),
        in_specs=[SMEM] * 3 + [HBM, VMEM],
        out_specs=VMEM,
        scratch_shapes=[pltpu.VMEM((rows, block_cols), jnp.bfloat16), pltpu.SemaphoreType.DMA],
        compiler_params=params(),
        cost_estimate=cost(),
        name="terms_b",
    )(ids, lengths, slot_job, grad_out, lax.all_gather(h_part, shards))
    grad_b = lax.psum_scatter(terms_b, "fsdp", scatter_dimension=0).astype(jnp.float32)
    middle = inside(middle + middle_in)

    result, far_out = base(0, None, ())
    parts = [lax.ppermute(far_out, "groups", SWAP)]
    last_out = last + far
    for c in range(1, len(CUTS)):
        result, far_out = base(c, result, (last_out,) if c == len(CUTS) - 1 and LATE else (terms_b,))
        parts.append(lax.ppermute(far_out, "groups", SWAP))
    for part, offset in zip(parts, offsets):
        result = place(result, part, ids, offset)
    grad_a = sum_terms(own_a, near, middle, outward(last_out))
    return result, grad_a[None], grad_b.T[None]


def local_any(activations, grad_out, codes, scales, adapter_a, adapter_b, lengths, slot_job):
    rows = activations.shape[0]
    width = activations.shape[1]
    wide = grad_out.shape[1]
    half = wide // 2
    both = adapter_a.shape[2]
    rank = both // 2
    jobs = lengths.shape[0]
    shards = lax.axis_size(("tp", "dp"))
    column = lax.axis_index(("tp", "dp"))
    block_cols = wide // shards
    first = lax.axis_index("fsdp") * rows
    starts = jnp.cumsum(lengths) - lengths
    positions = first + jnp.arange(rows, dtype=jnp.int32)
    row_job = jnp.sum((positions[:, None] >= starts[None, :]).astype(jnp.int32), axis=1) - 1
    onehot = row_job[:, None] == slot_job[None, :]
    scale_cols = jnp.repeat(jnp.repeat(scales, BLOCK, axis=0), BLOCK, axis=1)
    weight = (lax.all_gather(codes, "fsdp", axis=1, tiled=True).astype(jnp.float32) * scale_cols).astype(jnp.bfloat16)
    frozen = lax.dot_general(grad_out, weight, NT, preferred_element_type=jnp.float32)
    g_block = lax.dynamic_slice_in_dim(grad_out, column * block_cols, block_cols, 1)
    key_side = column * block_cols < half
    a_every = lax.all_gather(adapter_a, "fsdp", axis=0, tiled=True)
    b_every = lax.all_gather(adapter_b, "fsdp", axis=0, tiled=True)
    h_every = jnp.einsum("ri,sic->rsc", activations, a_every, preferred_element_type=jnp.float32)
    u_every = jnp.einsum("ro,sok->rsk", g_block, b_every, preferred_element_type=jnp.float32)
    h_part = jnp.sum(jnp.where(onehot[:, :, None], h_every, 0.0), axis=1)
    u_block = jnp.sum(jnp.where(onehot[:, :, None], u_every, 0.0), axis=1)
    u_part = jnp.concatenate([jnp.where(key_side, u_block, 0.0), jnp.where(key_side, 0.0, u_block)], axis=1)
    low_h = lax.psum(h_part.astype(jnp.bfloat16), ("tp", "dp"))
    low_u = lax.psum(u_part.astype(jnp.bfloat16), ("tp", "dp"))
    masked_u = jnp.where(onehot[:, :, None], low_u[:, None, :], 0).reshape(rows, jobs * both)
    branch = jnp.einsum("rsc,sic->ri", masked_u.reshape(rows, jobs, both), a_every, preferred_element_type=jnp.float32)
    input_gradient = (frozen + adapter_scale * branch).astype(jnp.bfloat16)
    h_side = jnp.where(key_side, low_h[:, :rank], low_h[:, rank:])
    masked_h = jnp.where(onehot[:, :, None], h_side[:, None, :], 0).reshape(rows, jobs * rank)
    down = lax.dot_general(activations, masked_u, TN, preferred_element_type=jnp.float32) * adapter_scale
    up = lax.dot_general(g_block, masked_h, TN, preferred_element_type=jnp.float32) * adapter_scale
    down = down.reshape(width, jobs, both).astype(jnp.bfloat16)
    up = up.reshape(block_cols, jobs, rank).astype(jnp.bfloat16)
    summed_a = lax.psum_scatter(down, "fsdp", scatter_dimension=1, tiled=True).astype(jnp.float32)
    summed_b = lax.psum_scatter(up, "fsdp", scatter_dimension=1, tiled=True).astype(jnp.float32)
    return input_gradient, jnp.transpose(summed_a, (1, 0, 2)), jnp.transpose(summed_b, (1, 0, 2))


def solution(mesh):
    in_specs = (
        P(("groups", "fsdp"), ("tp", "dp")),
        P(("groups", "fsdp"), None),
        P(("tp", "dp"), "fsdp"),
        P(("tp", "dp"), None),
        P("fsdp", ("tp", "dp"), None),
        P("fsdp", ("tp", "dp"), None),
        P("groups"),
        P(),
    )
    out_specs = (
        P(("groups", "fsdp"), ("tp", "dp")),
        P(("groups", "fsdp"), ("tp", "dp"), None),
        P(("groups", "fsdp"), ("tp", "dp"), None),
    )
    shape = dict(mesh.shape)
    chain = shape == {"groups": 2, "fsdp": 4, "tp": 2, "dp": 2}
    local = local_chain if chain else local_any
    return jax.shard_map(local, mesh=mesh, in_specs=in_specs, out_specs=out_specs, check_vma=False)
```

```python
import functools
import math
import jax
import jax.numpy as jnp
from jax import lax
from jax.experimental import pallas as pl
from jax.experimental.pallas import tpu as pltpu
from jax.sharding import PartitionSpec as P

BLOCK = 128
CUTS = (2, 3, 3)
SUM_COST = 20
LATE = True
BASE_COST = 0

adapter_scale = 2.0

SWAP = [(0, 1), (1, 0)]
NT = (((1,), (1,)), ((), ()))
TN = (((0,), (0,)), ((), ()))

HBM = pl.BlockSpec(memory_space=pltpu.HBM)
ANY = pl.BlockSpec(memory_space=pl.ANY)
SMEM = pl.BlockSpec(memory_space=pltpu.SMEM)
VMEM = pl.BlockSpec(memory_space=pltpu.VMEM)
VMEM_LIMIT = 48 * 1024 * 1024


def swap_groups(blocks, f, n):
    others = jnp.stack([lax.dynamic_index_in_dim(blocks, (f + k) % n, 0, keepdims=False) for k in range(1, n)])
    return lax.ppermute(others, "groups", SWAP)


def hold(x, after):
    return pl.pallas_call(
        lambda *refs: None,
        out_shape=jax.ShapeDtypeStruct(x.shape, x.dtype),
        in_specs=[HBM] * (1 + len(after)),
        out_specs=HBM,
        input_output_aliases={0: 0},
        cost_estimate=cost(),
        name="hold",
    )(x, *after)


def pack(a_own, codes, ids, size):
    half, both = a_own.shape[0] // 2, a_own.shape[1]
    parts = codes.shape[1] // both

    def kernel(ids, a_own, codes, out, held, sems, out_sems):
        first = pl.multiple_of(ids[1] * half, half)
        copies = [pltpu.make_async_copy(a_own.at[pl.ds(first, half)], held.at[pl.ds(0, half)], sems.at[parts])]
        for k in range(parts):
            src = codes.at[pl.ds(first, size), pl.ds(k * both, both)]
            copies.append(pltpu.make_async_copy(src, held.at[pl.ds(half + k * size, size)], sems.at[k]))
        places = [pl.ds(half + k * size, size) for k in range(parts)]
        places = [pl.ds(0, half)] + places
        stores = [pltpu.make_async_copy(held.at[place], out.at[place], out_sems.at[k]) for k, place in enumerate(places)]
        for copy in copies:
            copy.start()
        for copy, store in zip(copies, stores):
            copy.wait()
            store.start()
        for store in stores:
            store.wait()

    shape = (half + parts * size, both)
    return pl.pallas_call(
        kernel,
        out_shape=jax.ShapeDtypeStruct(shape, a_own.dtype),
        in_specs=[SMEM, HBM, HBM],
        out_specs=HBM,
        scratch_shapes=[pltpu.VMEM(shape, a_own.dtype), pltpu.SemaphoreType.DMA((parts + 1,)), pltpu.SemaphoreType.DMA((parts + 1,))],
        cost_estimate=cost(),
        name="pack",
    )(ids, a_own, codes)


def inward(x):
    return lax.ppermute(x, "fsdp", [(0, 1), (3, 2)])


def inside(x):
    return lax.ppermute(x, "fsdp", [(1, 2), (2, 1)])


def outward(x):
    return lax.ppermute(x, "fsdp", [(1, 0), (2, 3)])


def slot_bounds(slot, lengths, slot_job, first):
    job = slot_job[slot]
    start = jnp.int32(0)
    for j in range(lengths.shape[0]):
        start = start + jnp.where(j < job, lengths[j], 0)
    return start - first, start - first + lengths[job]


def row_mask(slot, lengths, slot_job, first, shape):
    low, high = slot_bounds(slot, lengths, slot_job, first)
    row = lax.broadcasted_iota(jnp.int32, shape, 0)
    return (row >= low) & (row < high)


def u_kernel(n, ids, lengths, slot_job, grad, factors, *refs):
    out, g_all, b_all, sems = refs[-4:]
    f, column = ids[0], ids[2]
    rows, cols = g_all.shape
    rank = out.shape[1]
    grab = pltpu.make_async_copy(grad.at[:, pl.ds(pl.multiple_of(column * cols, cols), cols)], g_all, sems.at[0])
    grab.start()
    fetch = pltpu.make_async_copy(factors, b_all, sems.at[1])
    fetch.start()
    fetch.wait()
    grab.wait()
    total = jnp.zeros(out.shape, jnp.float32)
    for s in range(n):
        part = lax.dot_general(g_all[...], b_all[s], NT, preferred_element_type=jnp.float32)
        total = jnp.where(row_mask(s, lengths, slot_job, f * rows, out.shape), part, total)
    out[...] = total.astype(out.dtype)


def fetch_other(slot, f, n, own, others, dst, sem):
    pl.when(f == slot)(lambda: pltpu.make_async_copy(own, dst, sem).start())
    pl.when(f != slot)(lambda: pltpu.make_async_copy(others.at[lax.rem(slot - f + 2 * n - 1, n)], dst, sem).start())


def h_kernel(n, ids, lengths, slot_job, acts, own, others, first_blocks, *refs):
    out, a_all, sems = refs[-3:]
    f, g = ids[0], ids[1]
    rows = acts.shape[0]
    half = own.shape[0] // 2
    both = out.shape[1]
    here, there = pl.multiple_of(g * half, half), pl.multiple_of((1 - g) * half, half)
    for s in range(n):
        dst = a_all.at[pl.ds(here, half), pl.ds(s * both, both)]
        pltpu.make_async_copy(first_blocks.at[s, pl.ds(0, half)], dst, sems.at[s, 0]).start()
        fetch_other(s, f, n, own.at[pl.ds(there, half)], others, a_all.at[pl.ds(there, half), pl.ds(s * both, both)], sems.at[s, 1])
    for s in range(n):
        for side in range(2):
            pltpu.make_async_copy(own.at[pl.ds(0, half)], a_all.at[pl.ds(0, half), pl.ds(s * both, both)], sems.at[s, side]).wait()
    product = jnp.dot(acts[...], a_all[...], preferred_element_type=jnp.float32)
    total = jnp.zeros(out.shape, jnp.float32)
    for s in range(n):
        total = jnp.where(row_mask(s, lengths, slot_job, f * rows, out.shape), product[:, s * both:(s + 1) * both], total)
    out[...] = total.astype(out.dtype)


def added(parts):
    total = parts[0].astype(jnp.float32)
    for part in parts[1:]:
        total = total + part.astype(jnp.float32)
    return total.astype(jnp.bfloat16)


def terms_a_kernel(n, ids, lengths, slot_job, acts, u_parts, masked, *refs):
    outs, (held, sems) = refs[:n], refs[n:]
    f = ids[0]
    shards, rows, _ = u_parts.shape
    both = held.shape[2]
    key = added([u_parts[k] for k in range(shards // 2)])
    value = added([u_parts[k] for k in range(shards // 2, shards)])
    doubled = jnp.concatenate([key, value], axis=1).astype(jnp.float32) * adapter_scale
    for s in range(n):
        part = jnp.where(row_mask(s, lengths, slot_job, f * rows, doubled.shape), doubled, 0.0).astype(jnp.bfloat16)
        masked[:, s * both:(s + 1) * both] = part
    left = f < n // 2
    third = jnp.where(f == 0, 1, jnp.where(f == n - 1, n - 2, jnp.where(left, 0, n - 1)))
    copies = [pltpu.make_async_copy(held.at[k], outs[k], sems.at[k]) for k in range(n)]
    for k, s in enumerate((jnp.where(left, n - 1, 0), jnp.where(left, n - 2, 1), third, f)):
        part = jnp.where(row_mask(s, lengths, slot_job, f * rows, doubled.shape), doubled, 0.0).astype(jnp.bfloat16)
        held[k] = lax.dot_general(acts[...], part, TN, preferred_element_type=jnp.float32).astype(jnp.bfloat16)
        copies[k].start()
    for copy in copies:
        copy.wait()


def terms_b_kernel(n, ids, lengths, slot_job, grad, h_parts, out, g_all, sem):
    f, column = ids[0], ids[2]
    rows, cols = g_all.shape
    shards = h_parts.shape[0]
    rank = out.shape[1]
    grab = pltpu.make_async_copy(grad.at[:, pl.ds(pl.multiple_of(column * cols, cols), cols)], g_all, sem)
    grab.start()
    low_h = added([h_parts[k] for k in range(shards)]).astype(jnp.float32) * adapter_scale
    side = jnp.where(column < shards // 2, low_h[:, :rank], low_h[:, rank:])
    grab.wait()
    for s in range(n):
        part = jnp.where(row_mask(s, lengths, slot_job, f * rows, side.shape), side, 0.0).astype(jnp.bfloat16)
        out[s] = lax.dot_general(part, g_all[...], TN, preferred_element_type=jnp.float32).astype(jnp.bfloat16)


def base_kernel(n, offset, size, packed, ids, grad, far_core, far_other, masked, far_masked, scale_rows, first_blocks, blocks, *refs):
    out, far_out, grads, masks, codes, factors, result, sems, in_sems, out_sem = refs[-10:]
    g, dp = ids[1], ids[3]
    rows, wide = grad.shape
    half, both, cols = out.shape[1] // 2, first_blocks.shape[2], wide // n
    part = far_core.shape[0]
    first = pl.multiple_of(g * half + offset, BLOCK)
    near = [
        pltpu.make_async_copy(grad, grads.at[pl.ds(0, rows)], in_sems.at[0]),
        pltpu.make_async_copy(masked, masks.at[pl.ds(0, rows)], in_sems.at[3]),
    ]
    far = [
        pltpu.make_async_copy(far_core, grads.at[pl.ds(pl.multiple_of(rows + dp * part, part), part)], in_sems.at[1]),
        pltpu.make_async_copy(far_other, grads.at[pl.ds(pl.multiple_of(rows + (1 - dp) * part, part), part)], in_sems.at[2]),
        pltpu.make_async_copy(far_masked, masks.at[pl.ds(rows, rows)], in_sems.at[4]),
    ]
    arriving = []
    for s in range(n):
        if packed:
            for k in range(cols // both):
                src = first_blocks.at[s, pl.ds(half + k * size, size)]
                arriving.append(pltpu.make_async_copy(src, codes.at[:, pl.ds(s * cols + k * both, both)], sems.at[s, k]))
        else:
            arriving.append(pltpu.make_async_copy(blocks.at[s], codes.at[:, pl.ds(s * cols, cols)], sems.at[s, 0]))
        near.append(pltpu.make_async_copy(first_blocks.at[s, pl.ds(offset, size)], factors.at[:, pl.ds(s * both, both)], sems.at[n, s]))
    for copy in arriving + near + far:
        copy.start()
    for copy in arriving:
        copy.wait()
    weight = []
    for b in range(size // BLOCK):
        scale = scale_rows[pl.ds(first // BLOCK + b, 1), :]
        weight.append((codes[b * BLOCK:(b + 1) * BLOCK, :].astype(jnp.float32) * scale).astype(jnp.bfloat16))
    weight = jnp.concatenate(weight, axis=0)

    def product(take):
        total = lax.dot_general(grads[take], weight, NT, preferred_element_type=jnp.float32)
        total += lax.dot_general(masks[take], factors[...], NT, preferred_element_type=jnp.float32)
        return total.astype(jnp.bfloat16)

    for copy in near:
        copy.wait()
    result[...] = product(slice(0, rows))
    keep = pltpu.make_async_copy(result, out.at[:, pl.ds(first, size)], out_sem)
    keep.start()
    for copy in far:
        copy.wait()
    far_out[...] = product(slice(rows, 2 * rows))
    keep.wait()


def params():
    return pltpu.CompilerParams(vmem_limit_bytes=VMEM_LIMIT)


def cost(us=0):
    return pl.CostEstimate(flops=int(us * 1.1e9) + 1, bytes_accessed=1, transcendentals=0)


def sum_terms(own, *arrived):
    def kernel(own, *refs):
        total = own[...].astype(jnp.float32)
        for ref in refs[:-1]:
            total = total + ref[...].astype(jnp.float32)
        refs[-1][...] = total

    return pl.pallas_call(
        kernel,
        out_shape=jax.ShapeDtypeStruct(own.shape, jnp.float32),
        compiler_params=params(),
        cost_estimate=cost(SUM_COST),
        name="sum_terms",
    )(own, *arrived)


def piece_of(whole, ids, offset, size, after):
    half = whole.shape[0] // 2
    step = math.gcd(math.gcd(offset, size), half)

    def kernel(ids, whole, *refs):
        refs[-1][...] = whole[...]

    return pl.pallas_call(
        kernel,
        out_shape=jax.ShapeDtypeStruct((size, whole.shape[1]), whole.dtype),
        grid_spec=pltpu.PrefetchScalarGridSpec(
            num_scalar_prefetch=1,
            grid=(size // step,),
            in_specs=[pl.BlockSpec((step, whole.shape[1]), lambda i, ids: ((ids[1] * half + offset) // step + i, 0))] + [HBM] * len(after),
            out_specs=pl.BlockSpec((step, whole.shape[1]), lambda i, ids: (i, 0)),
        ),
        cost_estimate=cost(),
        name="piece",
    )(ids, whole, *after)


def place(whole, part, ids, offset):
    def kernel(ids, part, _, out, sem):
        first = pl.multiple_of((1 - ids[1]) * (out.shape[1] // 2) + offset, BLOCK)
        copy = pltpu.make_async_copy(part, out.at[:, pl.ds(first, part.shape[1])], sem)
        copy.start()
        copy.wait()

    return pl.pallas_call(
        kernel,
        out_shape=jax.ShapeDtypeStruct(whole.shape, whole.dtype),
        in_specs=[SMEM, VMEM, HBM],
        out_specs=HBM,
        scratch_shapes=[pltpu.SemaphoreType.DMA],
        input_output_aliases={2: 0},
        compiler_params=params(),
        cost_estimate=cost(),
        name="place",
    )(ids, part, whole)


def local_chain(activations, grad_out, codes, scales, adapter_a, adapter_b, lengths, slot_job):
    n = 4
    rows, width = activations.shape
    wide = grad_out.shape[1]
    both = adapter_a.shape[2]
    rank = both // 2
    cols = codes.shape[1]
    block_cols = adapter_b.shape[1]
    half = width // 2
    f, g = lax.axis_index("fsdp"), lax.axis_index("groups")
    tp, dp = lax.axis_index("tp"), lax.axis_index("dp")
    ids = jnp.stack([f, g, tp * 2 + dp, dp]).astype(jnp.int32)
    a_own = adapter_a[0]
    shards = ("tp", "dp")

    b_all = lax.all_gather(adapter_b[0].T, "fsdp")
    part = rows // 2
    far_core = lax.ppermute(lax.dynamic_slice_in_dim(grad_out, dp * part, part, 0), "groups", SWAP)
    far_other = lax.ppermute(far_core, "dp", SWAP)

    sizes = [half * parts // sum(CUTS) for parts in CUTS]
    offsets = [sum(sizes[:c]) for c in range(len(CUTS))]
    first_blocks = lax.all_gather(pack(a_own, codes, ids, sizes[0]), "fsdp")
    code_blocks = [first_blocks] + [
        lax.all_gather(piece_of(codes, ids, offset, size, (b_all,)), "fsdp") for offset, size in zip(offsets[1:], sizes[1:])
    ]

    u_part = pl.pallas_call(
        functools.partial(u_kernel, n),
        out_shape=jax.ShapeDtypeStruct((rows, rank), jnp.bfloat16),
        in_specs=[SMEM] * 3 + [HBM] * 2,
        out_specs=VMEM,
        scratch_shapes=[
            pltpu.VMEM((rows, block_cols), jnp.bfloat16),
            pltpu.VMEM((n, rank, block_cols), jnp.bfloat16),
            pltpu.SemaphoreType.DMA((2,)),
        ],
        compiler_params=params(),
        cost_estimate=cost(),
        name="low_u",
    )(ids, lengths, slot_job, grad_out, b_all)
    masked_u, far, middle, last, own_a = pl.pallas_call(
        functools.partial(terms_a_kernel, n),
        out_shape=(jax.ShapeDtypeStruct((rows, n * both), jnp.bfloat16),) + (jax.ShapeDtypeStruct((width, both), jnp.bfloat16),) * 4,
        in_specs=[SMEM] * 3 + [VMEM] * 2,
        out_specs=(VMEM,) + (HBM,) * 4,
        scratch_shapes=[pltpu.VMEM((n, width, both), jnp.bfloat16), pltpu.SemaphoreType.DMA((n,))],
        compiler_params=params(),
        cost_estimate=cost(),
        name="terms_a",
    )(ids, lengths, slot_job, activations, lax.all_gather(u_part, shards))
    far_in, middle_in, near = inward(far), inward(middle), inward(last)
    far_masked = lax.ppermute(masked_u, "groups", SWAP)
    a_others = swap_groups(first_blocks[:, :half], f, n)
    far = inside(far + far_in)

    scale_rows = jnp.repeat(scales, BLOCK, axis=1)

    def base(c, before, after):
        blocks, offset, size = code_blocks[c], offsets[c], sizes[c]
        more = [] if before is None else [before]
        return pl.pallas_call(
            functools.partial(base_kernel, n, offset, size, c == 0),
            out_shape=(jax.ShapeDtypeStruct((rows, width), jnp.bfloat16), jax.ShapeDtypeStruct((rows, size), jnp.bfloat16)),
            in_specs=[SMEM] + [ANY] * 5 + [VMEM] + [HBM] * (2 + len(more)) + [ANY] * len(after),
            out_specs=(HBM, VMEM),
            scratch_shapes=[
                pltpu.VMEM((2 * rows, wide), jnp.bfloat16),
                pltpu.VMEM((2 * rows, n * both), jnp.bfloat16),
                pltpu.VMEM((size, wide), jnp.bfloat16),
                pltpu.VMEM((size, n * both), jnp.bfloat16),
                pltpu.VMEM((rows, size), jnp.bfloat16),
                pltpu.SemaphoreType.DMA((n + 1, wide // n // both)),
                pltpu.SemaphoreType.DMA((5,)),
                pltpu.SemaphoreType.DMA,
            ],
            input_output_aliases={9: 0} if more else {},
            compiler_params=params(),
            cost_estimate=cost(BASE_COST),
            name="base",
        )(ids, grad_out, far_core, far_other, masked_u, far_masked, scale_rows, first_blocks, blocks, *more, *after)

    h_part = pl.pallas_call(
        functools.partial(h_kernel, n),
        out_shape=jax.ShapeDtypeStruct((rows, both), jnp.bfloat16),
        in_specs=[SMEM] * 3 + [VMEM] + [ANY] * 3,
        out_specs=VMEM,
        scratch_shapes=[pltpu.VMEM((width, n * both), jnp.bfloat16), pltpu.SemaphoreType.DMA((n, 2))],
        compiler_params=params(),
        cost_estimate=cost(),
        name="low_h",
    )(ids, lengths, slot_job, activations, a_own, a_others, first_blocks)
    terms_b = pl.pallas_call(
        functools.partial(terms_b_kernel, n),
        out_shape=jax.ShapeDtypeStruct((n, rank, block_cols), jnp.bfloat16),
        in_specs=[SMEM] * 3 + [HBM, VMEM],
        out_specs=VMEM,
        scratch_shapes=[pltpu.VMEM((rows, block_cols), jnp.bfloat16), pltpu.SemaphoreType.DMA],
        compiler_params=params(),
        cost_estimate=cost(),
        name="terms_b",
    )(ids, lengths, slot_job, grad_out, lax.all_gather(h_part, shards))
    grad_b = lax.psum_scatter(terms_b, "fsdp", scatter_dimension=0).astype(jnp.float32)
    middle = inside(middle + middle_in)

    result, far_out = base(0, None, ())
    parts = [lax.ppermute(far_out, "groups", SWAP)]
    last_out = last + far
    for c in range(1, len(CUTS)):
        result, far_out = base(c, result, (last_out,) if c == len(CUTS) - 1 and LATE else (terms_b,))
        parts.append(lax.ppermute(far_out, "groups", SWAP))
    for part, offset in zip(parts, offsets):
        result = place(result, part, ids, offset)
    grad_a = sum_terms(own_a, near, middle, outward(last_out))
    return result, grad_a[None], grad_b.T[None]


def local_any(activations, grad_out, codes, scales, adapter_a, adapter_b, lengths, slot_job):
    rows = activations.shape[0]
    width = activations.shape[1]
    wide = grad_out.shape[1]
    half = wide // 2
    both = adapter_a.shape[2]
    rank = both // 2
    jobs = lengths.shape[0]
    shards = lax.axis_size(("tp", "dp"))
    column = lax.axis_index(("tp", "dp"))
    block_cols = wide // shards
    first = lax.axis_index("fsdp") * rows
    starts = jnp.cumsum(lengths) - lengths
    positions = first + jnp.arange(rows, dtype=jnp.int32)
    row_job = jnp.sum((positions[:, None] >= starts[None, :]).astype(jnp.int32), axis=1) - 1
    onehot = row_job[:, None] == slot_job[None, :]
    scale_cols = jnp.repeat(jnp.repeat(scales, BLOCK, axis=0), BLOCK, axis=1)
    weight = (lax.all_gather(codes, "fsdp", axis=1, tiled=True).astype(jnp.float32) * scale_cols).astype(jnp.bfloat16)
    frozen = lax.dot_general(grad_out, weight, NT, preferred_element_type=jnp.float32)
    g_block = lax.dynamic_slice_in_dim(grad_out, column * block_cols, block_cols, 1)
    key_side = column * block_cols < half
    a_every = lax.all_gather(adapter_a, "fsdp", axis=0, tiled=True)
    b_every = lax.all_gather(adapter_b, "fsdp", axis=0, tiled=True)
    h_every = jnp.einsum("ri,sic->rsc", activations, a_every, preferred_element_type=jnp.float32)
    u_every = jnp.einsum("ro,sok->rsk", g_block, b_every, preferred_element_type=jnp.float32)
    h_part = jnp.sum(jnp.where(onehot[:, :, None], h_every, 0.0), axis=1)
    u_block = jnp.sum(jnp.where(onehot[:, :, None], u_every, 0.0), axis=1)
    u_part = jnp.concatenate([jnp.where(key_side, u_block, 0.0), jnp.where(key_side, 0.0, u_block)], axis=1)
    low_h = lax.psum(h_part.astype(jnp.bfloat16), ("tp", "dp"))
    low_u = lax.psum(u_part.astype(jnp.bfloat16), ("tp", "dp"))
    masked_u = jnp.where(onehot[:, :, None], low_u[:, None, :], 0).reshape(rows, jobs * both)
    branch = jnp.einsum("rsc,sic->ri", masked_u.reshape(rows, jobs, both), a_every, preferred_element_type=jnp.float32)
    input_gradient = (frozen + adapter_scale * branch).astype(jnp.bfloat16)
    h_side = jnp.where(key_side, low_h[:, :rank], low_h[:, rank:])
    masked_h = jnp.where(onehot[:, :, None], h_side[:, None, :], 0).reshape(rows, jobs * rank)
    down = lax.dot_general(activations, masked_u, TN, preferred_element_type=jnp.float32) * adapter_scale
    up = lax.dot_general(g_block, masked_h, TN, preferred_element_type=jnp.float32) * adapter_scale
    down = down.reshape(width, jobs, both).astype(jnp.bfloat16)
    up = up.reshape(block_cols, jobs, rank).astype(jnp.bfloat16)
    summed_a = lax.psum_scatter(down, "fsdp", scatter_dimension=1, tiled=True).astype(jnp.float32)
    summed_b = lax.psum_scatter(up, "fsdp", scatter_dimension=1, tiled=True).astype(jnp.float32)
    return input_gradient, jnp.transpose(summed_a, (1, 0, 2)), jnp.transpose(summed_b, (1, 0, 2))


def solution(mesh):
    in_specs = (
        P(("groups", "fsdp"), ("tp", "dp")),
        P(("groups", "fsdp"), None),
        P(("tp", "dp"), "fsdp"),
        P(("tp", "dp"), None),
        P("fsdp", ("tp", "dp"), None),
        P("fsdp", ("tp", "dp"), None),
        P("groups"),
        P(),
    )
    out_specs = (
        P(("groups", "fsdp"), ("tp", "dp")),
        P(("groups", "fsdp"), ("tp", "dp"), None),
        P(("groups", "fsdp"), ("tp", "dp"), None),
    )
    shape = dict(mesh.shape)
    chain = shape == {"groups": 2, "fsdp": 4, "tp": 2, "dp": 2}
    local = local_chain if chain else local_any
    return jax.shard_map(local, mesh=mesh, in_specs=in_specs, out_specs=out_specs, check_vma=False)
```
